128 devices in a mesh: row: 4 (over y), col: 32 (over x, z, core).
Axes of the slice: x: 4, y: 4, z: 4, core: 2. Of those that a mesh axis runs over, the one named last changes fastest.
Arguments:
- specimen: float32 [2, 2048, 16384], P(None, 'row', 'col'), may hold values from -1 to 2, as said below
- probe_field: float32 [2, 256, 256], replicated, may hold values from -6 to 6
- measured: float32 [4, 32, 8, 256, 256], P('row', 'col'), may hold values from 0 to 4
- offsets: int32 [4, 32, 8, 2], P('row', 'col'), may hold values from 0 to 511
- live_counts: int32 [4, 32], P('row', 'col'), may hold values from 1 to 8, as said below
Outputs:
- specimen_grad: float32 [2, 2048, 16384], P(None, 'row', 'col')
- probe_step: float32 [2, 256, 256], replicated
The draws below stay inside these ranges and needn't reach their ends.
Inputs may be any that keep to these rules, and one draw needn't show every extreme that they name: `specimen`: real parts lie in 0.5 to 2 and imaginary parts in -1 to 1. `live_counts`: some device has all 8 slots live.
All inputs are finite; a program needn't handle non-finite values.
Results may differ from the reference program's by a relative error of at most 0.0003.
Values sent between devices are 32-bit elements; how exact they have to be, the bound alone decides.
A program may use at most 128 MiB of HBM per device.

```python
import math
import jax
import jax.numpy as jnp
from jax import lax

W = 256
TILE = 512
SLOTS = 8
NR = 2048
NC = 16384
N_ROW = 4
N_COL = 32


def draw_specimen(key, part):
    key_real = jax.random.fold_in(key, 11)
    key_imag = jax.random.fold_in(key, 12)
    real_part = jax.random.uniform(key_real, (NR, NC), jnp.float32, 0.5, 1.5)
    imag_part = jax.random.uniform(key_imag, (NR, NC), jnp.float32, -0.5, 0.5)
    return jnp.stack([real_part, imag_part]).astype(jnp.float32)


def draw_live_counts(key, part):
    key_counts = jax.random.fold_in(key, 21)
    key_pick = jax.random.fold_in(key, 22)
    counts = jax.random.randint(key_counts, (N_ROW * N_COL,), 1, SLOTS + 1, jnp.int32)
    chosen = jax.random.randint(key_pick, (), 0, N_ROW * N_COL, jnp.int32)
    counts = counts.at[chosen].set(SLOTS)
    return counts.reshape(N_ROW, N_COL)


def touch_ends(entries, rng, least, high):
    dims = entries.shape
    spot = [jax.random.randint(jax.random.fold_in(rng, axis), (), 0, dims[axis]) for axis in range(len(dims))]
    entries = entries.at[tuple(spot)].set(least)
    longest = dims.index(max(dims))
    spot[longest] = (spot[longest] + 1) % dims[longest]
    return entries.at[tuple(spot)].set(high)


def level_of(own_key, dims, split, least, top_value):
    def one(position, parts):
        draws = jax.random.uniform(jax.random.fold_in(jax.random.fold_in(own_key, 6), position), (parts,), jnp.float32, least / len(split), top_value / len(split))
        return jnp.repeat(jnp.exp(draws), dims[position] // parts).reshape((-1,) + (1,) * (len(dims) - position - 1))

    loudness = one(*split[0])
    for cut in split[1:]:
        loudness = loudness * one(*cut)
    return loudness


def gaussian(stream_key, extent, width, limit, kind=jnp.bfloat16):
    entries = width * jax.random.normal(stream_key, extent, jnp.float32)
    return jnp.clip(entries, min=-limit, max=limit).astype(kind)


def setup_inputs(seed: int = 0) -> dict:
    seeds = jax.random.split(jax.random.key(seed), 6)
    return {
        "specimen": draw_specimen(jax.random.fold_in(seeds[5], 71), 0),
        "probe_field": gaussian(seeds[1], (2, W, W), 1.0, 6.0, jnp.float32),
        "measured": jnp.clip(4.0 * jax.random.uniform(seeds[2], (N_ROW, N_COL, SLOTS, W, W), jnp.float32) ** level_of(seeds[2], (N_ROW, N_COL, SLOTS, W, W), ((0, 4), (1, 32)), -0.2, 0.2), 0.0, 4.0),
        "offsets": touch_ends(jax.random.randint(seeds[3], (N_ROW, N_COL, SLOTS, 2), 0, TILE), jax.random.fold_in(seeds[3], 1), 0, TILE - 1).astype(jnp.int32),
        "live_counts": draw_live_counts(jax.random.fold_in(seeds[5], 71), 0),
    }


near_field = 0.25

def chirp_phase():
    index_range = jnp.arange(W)
    wave_number = jnp.where(index_range < W // 2, index_range, index_range - W).astype(jnp.float32)
    squared = wave_number[:, None] ** 2 + wave_number[None, :] ** 2
    return -math.pi * near_field * squared / W

def reference(specimen, probe_field, measured, offsets, live_counts):
    whole = specimen[0] + 1j * specimen[1]
    probe_c = probe_field[0] + 1j * probe_field[1]
    phase = chirp_phase()
    forward_chirp = jnp.exp(1j * phase)
    backward_chirp = jnp.exp(-1j * phase)
    total = N_ROW * N_COL * SLOTS
    flat_index = jnp.arange(total).astype(jnp.int32)
    dev_row = flat_index // (N_COL * SLOTS)
    dev_col = flat_index // SLOTS % N_COL
    slot_index = flat_index % SLOTS
    flat_offsets = offsets.reshape(total, 2)
    flat_measured = measured.reshape(total, W, W)
    pixel = jnp.arange(W).astype(jnp.int32)

    def step(carry, batch_entry):
        grad_c, probe_sum, illum = carry
        row_delta, column_delta, slot_delta, patch_corner, observed_intensity = batch_entry
        row_idx = (row_delta * TILE + patch_corner[0] + pixel) % NR
        col_idx = (column_delta * TILE + patch_corner[1] + pixel) % NC
        window = whole[row_idx[:, None], col_idx[None, :]]
        active_mask = (slot_delta < live_counts[row_delta, column_delta]).astype(jnp.float32)
        wave = jnp.fft.ifft2(jnp.fft.fft2(probe_c * window) * forward_chirp)
        model_intensity = wave.real ** 2 + wave.imag ** 2
        amplitude_residual = active_mask * (model_intensity - observed_intensity)
        back = jnp.fft.ifft2(jnp.fft.fft2(amplitude_residual * wave) * backward_chirp)
        grad_c = grad_c.at[row_idx[:, None], col_idx[None, :]].add(jnp.conj(probe_c) * back)
        probe_sum = probe_sum + jnp.conj(window) * back
        illum = illum + active_mask * (window.real ** 2 + window.imag ** 2)
        return ((grad_c, probe_sum, illum), None)
    start = (jnp.zeros(whole.shape, whole.dtype), jnp.zeros(probe_c.shape, probe_c.dtype), jnp.zeros((W, W), jnp.float32))
    (grad_c, probe_sum, illum), _ = lax.scan(step, start, (dev_row, dev_col, slot_index, flat_offsets, flat_measured))
    specimen_grad = jnp.stack([grad_c.real, grad_c.imag])
    root = jnp.sqrt(illum)
    probe_step = jnp.stack([probe_sum.real / root, probe_sum.imag / root])
    return (specimen_grad, probe_step)
```

```python
import functools, math
import jax, jax.numpy as jnp, numpy as np, ml_dtypes
from jax import lax
from jax.experimental import pallas as pl
from jax.experimental.pallas import tpu as pltpu

W=256; T=512; S=8
BF=jnp.bfloat16
def tables():
    k=np.arange(W); k=np.where(k<W//2,k,k-W).astype(np.float64)
    h=np.exp(-1j*math.pi*0.25*k*k/W)
    a=np.fft.ifft(h)
    H=W//2
    d=(np.arange(H)[:,None]-np.arange(H)[None,:])
    out=[]
    for sgn in (1,-1):
        c=0.5*(a[d%W]+sgn*a[(d+H)%W])
        ml=np.block([[c.real,-c.imag],[c.imag,c.real]])
        out.append(ml)
    ml=np.stack(out)
    mr=np.swapaxes(ml,1,2)
    def split(m):
        hi=m.astype(np.float32).astype(ml_dtypes.bfloat16)
        lo=(m-hi.astype(np.float64)).astype(np.float32).astype(ml_dtypes.bfloat16)
        return hi,lo
    lh,ll=split(ml); rh,rl=split(mr)
    left=np.stack([np.concatenate([h_,h_,l_],axis=-1) for h_,l_ in ((lh,ll),(rh,rl))])
    right=np.stack([np.concatenate([h_,l_,h_],axis=-2) for h_,l_ in ((rh,rl),(lh,ll))])
    return left,right

def split(x):
    hi=x.astype(BF)
    lo=(x-hi.astype(jnp.float32)).astype(BF)
    return hi,lo

def right_mul(xr,xi,tab_ref,which):
    H=W//2
    outs=[]
    for n,(r,i) in enumerate(((xr[:,:H]+xr[:,H:],xi[:,:H]+xi[:,H:]),(xr[:,:H]-xr[:,H:],xi[:,:H]-xi[:,H:]))):
        s=jnp.concatenate([r,i],axis=1)
        hi,lo=split(s)
        lhs=jnp.concatenate([hi,hi,lo],axis=1)
        outs.append(jnp.dot(lhs,tab_ref[which,n],preferred_element_type=jnp.float32))
    u,v=outs
    yr=jnp.concatenate([u[:,:H]+v[:,:H],u[:,:H]-v[:,:H]],axis=1)
    yi=jnp.concatenate([u[:,H:]+v[:,H:],u[:,H:]-v[:,H:]],axis=1)
    return yr,yi

def left_mul(xr,xi,tab_ref,which):
    H=W//2
    outs=[]
    for n,(r,i) in enumerate(((xr[:H]+xr[H:],xi[:H]+xi[H:]),(xr[:H]-xr[H:],xi[:H]-xi[H:]))):
        s=jnp.concatenate([r,i],axis=0)
        hi,lo=split(s)
        rhs=jnp.concatenate([hi,lo,hi],axis=0)
        outs.append(jnp.dot(tab_ref[which,n],rhs,preferred_element_type=jnp.float32))
    u,v=outs
    yr=jnp.concatenate([u[:H]+v[:H],u[:H]-v[:H]],axis=0)
    yi=jnp.concatenate([u[H:]+v[H:],u[H:]-v[H:]],axis=0)
    return yr,yi

def kernel(offs,live,tile,right,below,corner,probe,meas,lt,rt, G,Rs,Bs,Cs,pg, ext,grad,mv,sem):
    H=W//2
    cps=[]
    for cb in range(6):
        for (top) in (True,False):
            if cb<4: src=(tile if top else below).at[:,:,pl.ds(128*cb,128)]
            else: src=(right if top else corner).at[:,:,pl.ds(128*(cb-4),128)]
            dst=ext.at[:,cb,pl.ds(0,512),:] if top else ext.at[:,cb,pl.ds(512,256),:]
            cps.append(pltpu.make_async_copy(src,dst,sem.at[len(cps)]))
    cps.append(pltpu.make_async_copy(meas,mv,sem.at[len(cps)]))
    for c in cps: c.start()
    grad[...]=jnp.zeros_like(grad)
    pg[...]=jnp.zeros_like(pg)
    for c in cps: c.wait()
    lane=lax.broadcasted_iota(jnp.int32,(W,128),1)
    def slot(s,_):
        r0=offs[2*s]; c0=offs[2*s+1]
        q=c0//128; sh=c0-q*128
        keep=lane<128-sh
        o=[]
        for ch in range(2):
            x=[pltpu.roll(ext[ch,q+j,pl.ds(r0,W),:],128-sh,1) for j in range(3)]
            o.append(jnp.concatenate([jnp.where(keep,x[0],x[1]),jnp.where(keep,x[1],x[2])],axis=1))
        orr,oi=o
        pr=probe[0]; pi=probe[1]
        ar=pr*orr-pi*oi; ai=pr*oi+pi*orr
        ar,ai=right_mul(ar,ai,rt,0)
        ar,ai=left_mul(ar,ai,lt,0)
        res=ar*ar+ai*ai-mv[s]
        ar,ai=right_mul(res*ar,res*ai,rt,1)
        br,bi=left_mul(ar,ai,lt,1)
        pg[0]+=orr*br+oi*bi
        pg[1]+=orr*bi-oi*br
        pg[2]+=orr*orr+oi*oi
        gr=pr*br+pi*bi; gi=pr*bi-pi*br
        low=lane<sh
        for ch,g in enumerate((gr,gi)):
            a=pltpu.roll(g[:,:128],sh,1); b=pltpu.roll(g[:,128:],sh,1)
            z=jnp.zeros_like(a)
            grad[ch,q,pl.ds(r0,W),:]+=jnp.where(low,z,a)
            grad[ch,q+1,pl.ds(r0,W),:]+=jnp.where(low,a,b)
            grad[ch,q+2,pl.ds(r0,W),:]+=jnp.where(low,b,z)
        return 0
    lax.fori_loop(0,live[0],slot,0)
    cps=[]
    for cb in range(6):
        for (top) in (True,False):
            if cb<4: src=(G if top else Bs).at[:,:,pl.ds(128*cb,128)]
            else: src=(Rs if top else Cs).at[:,:,pl.ds(128*(cb-4),128)]
            dst=grad.at[:,cb,pl.ds(0,512),:] if top else grad.at[:,cb,pl.ds(512,256),:]
            cps.append(pltpu.make_async_copy(dst,src,sem.at[len(cps)]))
    for c in cps: c.start()
    for c in cps: c.wait()

def compute(offs,live,tile,right,below,corner,probe,meas):
    f=jnp.float32
    left,rightt=tables()
    sd=jax.ShapeDtypeStruct
    A=pl.BlockSpec(memory_space=pl.ANY); V=pl.BlockSpec(memory_space=pltpu.VMEM); M=pl.BlockSpec(memory_space=pltpu.SMEM)
    return pl.pallas_call(kernel,
        out_shape=[sd((2,T,T),f),sd((2,T,W),f),sd((2,W,T),f),sd((2,W,W),f),sd((3,W,W),f)],
        in_specs=[M,M,A,A,A,A,V,A,V,V],out_specs=[A,A,A,A,V],
        scratch_shapes=[pltpu.VMEM((2,6,768,128),f),pltpu.VMEM((2,6,768,128),f),pltpu.VMEM((S,W,W),f),pltpu.SemaphoreType.DMA((13,))],
        compiler_params=pltpu.CompilerParams(vmem_limit_bytes=58*2**20),
    )(offs.reshape(-1),live.reshape(-1),tile,right,below,corner,probe,meas,jnp.asarray(left),jnp.asarray(rightt))


def passed_along(value, axis, by):
    devices = lax.axis_size(axis)
    return lax.ppermute(value, axis, [(i, (i + by) % devices) for i in range(devices)])


def local(specimen, probe_field, measured, offsets, live_counts):
    right = passed_along(specimen[:, :, :W], "col", -1)
    below = passed_along(specimen[:, :W, :], "row", -1)
    corner = passed_along(below[:, :, :W], "col", -1)
    G, Rs, Bs, Cs, pg = compute(offsets, live_counts, specimen, right, below, corner, probe_field, measured[0, 0])
    total = lax.psum(pg, ("row", "col"))
    spill_corner = passed_along(Cs, "col", 1)
    spill_right = passed_along(Rs, "col", 1)
    spill_below = passed_along(Bs.at[:, :, :W].add(spill_corner), "row", 1)
    grad = G.at[:, :, :W].add(spill_right).at[:, :W, :].add(spill_below)
    step = total[:2] / jnp.sqrt(total[2:])
    return (grad, step)


def solution(mesh):
    from jax.sharding import PartitionSpec as P
    in_specs = (P(None, "row", "col"), P(), P("row", "col", None, None, None), P("row", "col", None, None), P("row", "col"))
    out_specs = (P(None, "row", "col"), P())
    return jax.shard_map(local, mesh=mesh, in_specs=in_specs, out_specs=out_specs, check_vma=False)
```

```python
import functools, math
import jax, jax.numpy as jnp, numpy as np, ml_dtypes
from jax import lax
from jax.experimental import pallas as pl
from jax.experimental.pallas import tpu as pltpu

W=256; T=512; S=8
BF=jnp.bfloat16
def tables():
    k=np.arange(W); k=np.where(k<W//2,k,k-W).astype(np.float64)
    h=np.exp(-1j*math.pi*0.25*k*k/W)
    a=np.fft.ifft(h)
    H=W//2
    d=(np.arange(H)[:,None]-np.arange(H)[None,:])
    out=[]
    for sgn in (1,-1):
        c=0.5*(a[d%W]+sgn*a[(d+H)%W])
        ml=np.block([[c.real,-c.imag],[c.imag,c.real]])
        out.append(ml)
    ml=np.stack(out)
    mr=np.swapaxes(ml,1,2)
    def split(m):
        hi=m.astype(np.float32).astype(ml_dtypes.bfloat16)
        lo=(m-hi.astype(np.float64)).astype(np.float32).astype(ml_dtypes.bfloat16)
        return hi,lo
    lh,ll=split(ml); rh,rl=split(mr)
    left=np.stack([np.concatenate([h_,h_,l_],axis=-1) for h_,l_ in ((lh,ll),(rh,rl))])
    right=np.stack([np.concatenate([h_,l_,h_],axis=-2) for h_,l_ in ((rh,rl),(lh,ll))])
    return left,right

def split(x):
    hi=x.astype(BF)
    lo=(x-hi.astype(jnp.float32)).astype(BF)
    return hi,lo

def right_mul(xr,xi,tab_ref,which):
    H=W//2
    outs=[]
    for n,(r,i) in enumerate(((xr[:,:H]+xr[:,H:],xi[:,:H]+xi[:,H:]),(xr[:,:H]-xr[:,H:],xi[:,:H]-xi[:,H:]))):
        s=jnp.concatenate([r,i],axis=1)
        hi,lo=split(s)
        lhs=jnp.concatenate([hi,hi,lo],axis=1)
        outs.append(jnp.dot(lhs,tab_ref[which,n],preferred_element_type=jnp.float32))
    u,v=outs
    yr=jnp.concatenate([u[:,:H]+v[:,:H],u[:,:H]-v[:,:H]],axis=1)
    yi=jnp.concatenate([u[:,H:]+v[:,H:],u[:,H:]-v[:,H:]],axis=1)
    return yr,yi

def left_mul(xr,xi,tab_ref,which):
    H=W//2
    outs=[]
    for n,(r,i) in enumerate(((xr[:H]+xr[H:],xi[:H]+xi[H:]),(xr[:H]-xr[H:],xi[:H]-xi[H:]))):
        s=jnp.concatenate([r,i],axis=0)
        hi,lo=split(s)
        rhs=jnp.concatenate([hi,lo,hi],axis=0)
        outs.append(jnp.dot(tab_ref[which,n],rhs,preferred_element_type=jnp.float32))
    u,v=outs
    yr=jnp.concatenate([u[:H]+v[:H],u[:H]-v[:H]],axis=0)
    yi=jnp.concatenate([u[H:]+v[H:],u[H:]-v[H:]],axis=0)
    return yr,yi

def kernel(offs,live,tile,right,below,corner,probe,meas,lt,rt, G,Rs,Bs,Cs,pg, ext,grad,mv,sem):
    H=W//2
    cps=[]
    for cb in range(6):
        for (top) in (True,False):
            if cb<4: src=(tile if top else below).at[:,:,pl.ds(128*cb,128)]
            else: src=(right if top else corner).at[:,:,pl.ds(128*(cb-4),128)]
            dst=ext.at[:,cb,pl.ds(0,512),:] if top else ext.at[:,cb,pl.ds(512,256),:]
            cps.append(pltpu.make_async_copy(src,dst,sem.at[len(cps)]))
    cps.append(pltpu.make_async_copy(meas,mv,sem.at[len(cps)]))
    for c in cps: c.start()
    grad[...]=jnp.zeros_like(grad)
    pg[...]=jnp.zeros_like(pg)
    for c in cps: c.wait()
    lane=lax.broadcasted_iota(jnp.int32,(W,128),1)
    def slot(s,_):
        r0=offs[2*s]; c0=offs[2*s+1]
        q=c0//128; sh=c0-q*128
        keep=lane<128-sh
        o=[]
        for ch in range(2):
            x=[pltpu.roll(ext[ch,q+j,pl.ds(r0,W),:],128-sh,1) for j in range(3)]
            o.append(jnp.concatenate([jnp.where(keep,x[0],x[1]),jnp.where(keep,x[1],x[2])],axis=1))
        orr,oi=o
        pr=probe[0]; pi=probe[1]
        ar=pr*orr-pi*oi; ai=pr*oi+pi*orr
        ar,ai=right_mul(ar,ai,rt,0)
        ar,ai=left_mul(ar,ai,lt,0)
        res=ar*ar+ai*ai-mv[s]
        ar,ai=right_mul(res*ar,res*ai,rt,1)
        br,bi=left_mul(ar,ai,lt,1)
        pg[0]+=orr*br+oi*bi
        pg[1]+=orr*bi-oi*br
        pg[2]+=orr*orr+oi*oi
        gr=pr*br+pi*bi; gi=pr*bi-pi*br
        low=lane<sh
        for ch,g in enumerate((gr,gi)):
            a=pltpu.roll(g[:,:128],sh,1); b=pltpu.roll(g[:,128:],sh,1)
            z=jnp.zeros_like(a)
            grad[ch,q,pl.ds(r0,W),:]+=jnp.where(low,z,a)
            grad[ch,q+1,pl.ds(r0,W),:]+=jnp.where(low,a,b)
            grad[ch,q+2,pl.ds(r0,W),:]+=jnp.where(low,b,z)
        return 0
    lax.fori_loop(0,live[0],slot,0)
    cps=[]
    for cb in range(6):
        for (top) in (True,False):
            if cb<4: src=(G if top else Bs).at[:,:,pl.ds(128*cb,128)]
            else: src=(Rs if top else Cs).at[:,:,pl.ds(128*(cb-4),128)]
            dst=grad.at[:,cb,pl.ds(0,512),:] if top else grad.at[:,cb,pl.ds(512,256),:]
            cps.append(pltpu.make_async_copy(dst,src,sem.at[len(cps)]))
    for c in cps: c.start()
    for c in cps: c.wait()

def compute(offs,live,tile,right,below,corner,probe,meas):
    f=jnp.float32
    left,rightt=tables()
    sd=jax.ShapeDtypeStruct
    A=pl.BlockSpec(memory_space=pl.ANY); V=pl.BlockSpec(memory_space=pltpu.VMEM); M=pl.BlockSpec(memory_space=pltpu.SMEM)
    return pl.pallas_call(kernel,
        out_shape=[sd((2,T,T),f),sd((2,T,W),f),sd((2,W,T),f),sd((2,W,W),f),sd((3,W,W),f)],
        in_specs=[M,M,A,A,A,A,V,A,V,V],out_specs=[A,A,A,A,V],
        scratch_shapes=[pltpu.VMEM((2,6,768,128),f),pltpu.VMEM((2,6,768,128),f),pltpu.VMEM((S,W,W),f),pltpu.SemaphoreType.DMA((13,))],
        compiler_params=pltpu.CompilerParams(vmem_limit_bytes=58*2**20),
    )(offs.reshape(-1),live.reshape(-1),tile,right,below,corner,probe,meas,jnp.asarray(left),jnp.asarray(rightt))


MESH = pl.DeviceIdType.MESH


def put(src, dst, send, recv, device):
    return pltpu.make_async_remote_copy(src_ref=src, dst_ref=dst, send_sem=send, recv_sem=recv, device_id=device, device_id_type=MESH)


def places():
    row, col = lax.axis_index("row"), lax.axis_index("col")
    rows, cols = lax.axis_size("row"), lax.axis_size("col")
    return row, col, ((row + rows - 1) % rows, col), ((row + 1) % rows, col), (row, (col + cols - 1) % cols), (row, (col + 1) % cols)


def greet(devices):
    barrier = pltpu.get_barrier_semaphore()
    for device in devices:
        pl.semaphore_signal(barrier, inc=1, device_id=device, device_id_type=MESH)
    return barrier


def halo_kernel(tile, R, B, X, hop1, hop2, snd, rcv):
    row, col, up, down, left, right = places()
    pl.semaphore_wait(greet((up, down, left, right)), 4)
    n = [0]

    def send(src, dst, device):
        k = n[0]
        n[0] += 1
        c = put(src, dst, snd.at[k], rcv.at[k], device)
        c.start()
        return c

    H = W // 2
    Q = H // 2
    near = [pl.ds(H * k, H) for k in range(2)]
    far = [pl.ds(H + Q * k, Q) for k in range(2)]
    lo, hi = pl.ds(0, W), pl.ds(W, W)
    first = [send(tile.at[:, far[k], hi], hop1.at[k], down) for k in range(2)]
    b = [send(tile.at[:, near[k], lo], B.at[:, near[k], lo], up) for k in range(2)]
    r = send(tile.at[:, :, lo], R, left)
    b2 = send(tile.at[:, near[0], hi], B.at[:, near[0], hi], up)
    second, third, x = [], [], []
    for k in range(2):
        first[k].wait_recv()
        second.append(send(hop1.at[k], hop2.at[k], down))
    for k in range(2):
        b[k].wait_recv()
        x.append(send(B.at[:, near[k], lo], X.at[:, near[k], :], left))
        second[k].wait_recv()
        third.append(send(hop2.at[k], B.at[:, far[k], hi], down))
    for c in (r, b2, *third, *x):
        c.wait_recv()
    for c in (*first, *b, r, b2, *second, *third, *x):
        c.wait_send()


def halos(tile):
    f = jnp.float32
    A = pl.BlockSpec(memory_space=pl.ANY)
    sd = jax.ShapeDtypeStruct
    return pl.pallas_call(halo_kernel, out_shape=[sd((2, T, W), f), sd((2, W, T), f), sd((2, W, W), f)],
        in_specs=[A], out_specs=[A, A, A],
        scratch_shapes=[pltpu.VMEM((2, 2, W // 4, W), f), pltpu.VMEM((2, 2, W // 4, W), f), pltpu.SemaphoreType.DMA((12,)), pltpu.SemaphoreType.DMA((12,))],
        compiler_params=pltpu.CompilerParams(collective_id=0, has_side_effects=True, vmem_limit_bytes=58*2**20))(tile)


def spill_kernel(Rs, Bs, Cs, pg, RR, BR, step, hop1, hop2, corner, bleft, mine, half, acc, plane, part, ybuf, shard, loc, snd, rcv, psnd, prcv, gsnd, grcv):
    row, col, up, down, left, right = places()
    rows, chips = lax.axis_size("row"), lax.axis_size("col") // 2
    core, chip = col % 2, col // 2
    sib = (row, col + 1 - 2 * core)
    H = W // 2
    Q = H // 2
    step_rows = H // chips

    def peer(j):
        return (row, ((chip + j) % chips) * 2 + core)

    barrier = greet((up, down, left, right, sib, ((row + 2) % rows, col)))

    def hello(j, _):
        pl.semaphore_signal(barrier, inc=1, device_id=peer(j), device_id_type=MESH)
        return 0

    lax.fori_loop(1, chips, hello, 0)
    bl = pltpu.make_async_copy(Bs.at[:, :, pl.ds(0, W)], bleft, loc.at[0])
    bl.start()
    ml = pltpu.make_async_copy(pg.at[:, pl.ds(core * H, H), :], mine, loc.at[1])
    ml.start()
    pl.semaphore_wait(barrier, 6 + chips - 1)
    n = [0]

    def send(src, dst, device):
        k = n[0]
        n[0] += 1
        c = put(src, dst, snd.at[k], rcv.at[k], device)
        c.start()
        return c

    near = [pl.ds(H * k, H) for k in range(2)]
    far = [pl.ds(H + Q * k, Q) for k in range(2)]
    lo, hi = pl.ds(0, W), pl.ds(W, W)
    s1 = send(pg.at[:, pl.ds((1 - core) * H, H), :], half, sib)
    sc = send(Cs, corner, right)
    first = [send(Bs.at[:, far[k], hi], hop1.at[k], up) for k in range(2)]
    b2 = send(Bs.at[:, near[0], hi], BR.at[:, near[0], hi], down)
    ml.wait()
    s1.wait_recv()
    acc[...] = mine[...] + half[...]

    def shard_of(j):
        p = (chip + j) % chips
        return put(acc.at[:, pl.ds(pl.multiple_of(p * step_rows, step_rows), step_rows), :], plane.at[j], psnd.at[j], prcv.at[j], peer(j))

    def begin(j, _):
        shard_of(j).start()
        return 0

    lax.fori_loop(1, chips, begin, 0)
    r = send(Rs, RR, right)
    second, third = [], []
    for k in range(2):
        first[k].wait_recv()
        second.append(send(hop1.at[k], hop2.at[k], up))
    bl.wait()
    sc.wait_recv()
    bleft[...] += corner[...]
    b = send(bleft, BR.at[:, :, lo], down)

    part[...] = acc[:, pl.ds(pl.multiple_of(chip * step_rows, step_rows), step_rows), :]

    def collect(j, _):
        shard_of(j).wait_recv()
        part[...] += plane[j]
        return 0

    lax.fori_loop(1, chips, collect, 0)
    ys = [send(part, ybuf.at[row], ((row + k) % rows, col)) for k in range(1, 4)]
    ybuf[pl.ds(row, 1)] = part[...][None]
    for k in range(2):
        second[k].wait_recv()
        third.append(send(hop2.at[k], BR.at[:, far[k], hi], up))
    for y in ys:
        y.wait_recv()
    total = ybuf[0] + ybuf[1] + ybuf[2] + ybuf[3]
    shard[...] = total[:2] / jnp.sqrt(total[2:])

    here = pl.ds(pl.multiple_of(core * H + chip * step_rows, step_rows), step_rows)
    own = pltpu.make_async_copy(shard, step.at[:, here, :], loc.at[2])
    own.start()

    def gather(j):
        return put(shard, step.at[:, here, :], gsnd.at[j], grcv.at[j], peer(j))

    def begin2(j, _):
        gather(j).start()
        return 0

    lax.fori_loop(1, chips, begin2, 0)

    def collect2(j, _):
        gather(j).wait_recv()
        return 0

    lax.fori_loop(1, chips, collect2, 0)
    own.wait()
    mine_rows = pl.ds(pl.multiple_of(core * H, H), H)
    s5 = send(step.at[:, mine_rows, :], step.at[:, mine_rows, :], sib)
    for c in (r, b2, b, *third, s5):
        c.wait_recv()

    def drain(j, _):
        shard_of(j).wait_send()
        gather(j).wait_send()
        return 0

    lax.fori_loop(1, chips, drain, 0)
    for c in (s1, sc, r, b2, b, *first, *second, *third, *ys, s5):
        c.wait_send()


def spills(Rs, Bs, Cs, pg, rows, cols):
    f = jnp.float32
    chips = cols // 2
    A = pl.BlockSpec(memory_space=pl.ANY)
    sd = jax.ShapeDtypeStruct
    V = pltpu.VMEM
    D = pltpu.SemaphoreType.DMA
    sh = W // 2 // chips
    return pl.pallas_call(spill_kernel, out_shape=[sd((2, T, W), f), sd((2, W, T), f), sd((2, W, W), f)],
        in_specs=[A] * 4, out_specs=[A, A, A],
        scratch_shapes=[V((2, 2, W // 4, W), f), V((2, 2, W // 4, W), f), V((2, W, W), f), V((2, W, W), f),
            V((3, W // 2, W), f), V((3, W // 2, W), f), V((3, W // 2, W), f), V((chips, 3, sh, W), f), V((3, sh, W), f), V((rows, 3, sh, W), f), V((2, sh, W), f),
            D((3,)), D((15,)), D((15,)), D((chips,)), D((chips,)), D((chips,)), D((chips,))],
        compiler_params=pltpu.CompilerParams(collective_id=1, has_side_effects=True, vmem_limit_bytes=58*2**20))(Rs, Bs, Cs, pg)


def local(specimen, probe_field, measured, offsets, live_counts):
    right, below, corner = halos(specimen)
    G, Rs, Bs, Cs, pg = compute(offsets, live_counts, specimen, right, below, corner, probe_field, measured[0, 0])
    from_left, from_above, step = spills(Rs, Bs, Cs, pg, lax.axis_size("row"), lax.axis_size("col"))
    grad = G.at[:, :, :W].add(from_left).at[:, :W, :].add(from_above)
    return (grad, step)


def solution(mesh):
    from jax.sharding import PartitionSpec as P
    in_specs = (P(None, "row", "col"), P(), P("row", "col", None, None, None), P("row", "col", None, None), P("row", "col"))
    out_specs = (P(None, "row", "col"), P())
    return jax.shard_map(local, mesh=mesh, in_specs=in_specs, out_specs=out_specs, check_vma=False)
```

```python
import functools, math
import jax, jax.numpy as jnp, numpy as np, ml_dtypes
from jax import lax
from jax.experimental import pallas as pl
from jax.experimental.pallas import tpu as pltpu

W=256; T=512; S=8
VM2=24
BF=jnp.bfloat16
def tables():
    k=np.arange(W); k=np.where(k<W//2,k,k-W).astype(np.float64)
    h=np.exp(-1j*math.pi*0.25*k*k/W)
    a=np.fft.ifft(h)
    H=W//2
    d=(np.arange(H)[:,None]-np.arange(H)[None,:])
    out=[]
    for sgn in (1,-1):
        c=0.5*(a[d%W]+sgn*a[(d+H)%W])
        ml=np.block([[c.real,-c.imag],[c.imag,c.real]])
        out.append(ml)
    ml=np.stack(out)
    mr=np.swapaxes(ml,1,2)
    def split(m):
        hi=m.astype(np.float32).astype(ml_dtypes.bfloat16)
        lo=(m-hi.astype(np.float64)).astype(np.float32).astype(ml_dtypes.bfloat16)
        return hi,lo
    lh,ll=split(ml); rh,rl=split(mr)
    return np.stack([lh,rh]),np.stack([ll,rl])

def split(x):
    hi=x.astype(BF)
    lo=(x-hi.astype(jnp.float32)).astype(BF)
    return hi,lo

def right_mul(xr,xi,th,tl,which):
    H=W//2
    outs=[]
    for n,(r,i) in enumerate(((xr[:,:H]+xr[:,H:],xi[:,:H]+xi[:,H:]),(xr[:,:H]-xr[:,H:],xi[:,:H]-xi[:,H:]))):
        s=jnp.concatenate([r,i],axis=1)
        hi,lo=split(s)
        lhs=jnp.concatenate([hi,hi,lo],axis=1)
        outs.append(jnp.dot(lhs,jnp.concatenate([th[1-which,n],tl[1-which,n],th[1-which,n]],axis=0),preferred_element_type=jnp.float32))
    u,v=outs
    yr=jnp.concatenate([u[:,:H]+v[:,:H],u[:,:H]-v[:,:H]],axis=1)
    yi=jnp.concatenate([u[:,H:]+v[:,H:],u[:,H:]-v[:,H:]],axis=1)
    return yr,yi

def left_mul(xr,xi,th,tl,which):
    H=W//2
    outs=[]
    for n,(r,i) in enumerate(((xr[:H]+xr[H:],xi[:H]+xi[H:]),(xr[:H]-xr[H:],xi[:H]-xi[H:]))):
        s=jnp.concatenate([r,i],axis=0)
        hi,lo=split(s)
        rhs=jnp.concatenate([hi,lo,hi],axis=0)
        outs.append(jnp.dot(jnp.concatenate([th[which,n],th[which,n],tl[which,n]],axis=1),rhs,preferred_element_type=jnp.float32))
    u,v=outs
    yr=jnp.concatenate([u[:H]+v[:H],u[:H]-v[:H]],axis=0)
    yi=jnp.concatenate([u[H:]+v[H:],u[H:]-v[H:]],axis=0)
    return yr,yi

def kernel(offs,live,ext,probe,mv,th,tl, grad,pg):
    grad[...]=jnp.zeros_like(grad)
    pg[...]=jnp.zeros_like(pg)
    lane=lax.broadcasted_iota(jnp.int32,(W,128),1)
    def slot(s,_):
        r0=offs[0,0,0,s]; c0=offs[0,0,1,s]
        q=c0//128; sh=c0-q*128
        keep=lane<128-sh
        o=[]
        for ch in range(2):
            x=[pltpu.roll(ext[ch,q+j,pl.ds(r0,W),:],128-sh,1) for j in range(3)]
            o.append(jnp.concatenate([jnp.where(keep,x[0],x[1]),jnp.where(keep,x[1],x[2])],axis=1))
        orr,oi=o
        pr=probe[0]; pi=probe[1]
        ar=pr*orr-pi*oi; ai=pr*oi+pi*orr
        ar,ai=right_mul(ar,ai,th,tl,0)
        ar,ai=left_mul(ar,ai,th,tl,0)
        res=ar*ar+ai*ai-mv[s]
        ar,ai=right_mul(res*ar,res*ai,th,tl,1)
        br,bi=left_mul(ar,ai,th,tl,1)
        pg[0]+=orr*br+oi*bi
        pg[1]+=orr*bi-oi*br
        pg[2]+=orr*orr+oi*oi
        gr=pr*br+pi*bi; gi=pr*bi-pi*br
        low=lane<sh
        for ch,g in enumerate((gr,gi)):
            a=pltpu.roll(g[:,:128],sh,1); b=pltpu.roll(g[:,128:],sh,1)
            z=jnp.zeros_like(a)
            grad[ch,q,pl.ds(r0,W),:]+=jnp.where(low,z,a)
            grad[ch,q+1,pl.ds(r0,W),:]+=jnp.where(low,a,b)
            grad[ch,q+2,pl.ds(r0,W),:]+=jnp.where(low,b,z)
        return 0
    lax.fori_loop(0,live[0,0],slot,0)


def compute(offs,live,ext,probe,meas,hi,lo):
    f=jnp.float32
    sd=jax.ShapeDtypeStruct
    V=pl.BlockSpec(memory_space=pltpu.VMEM); M=pl.BlockSpec(memory_space=pltpu.SMEM)
    return pl.pallas_call(kernel,
        out_shape=[sd((2,6,T+W,128),f),sd((3,W,W),f)],
        in_specs=[M,M,V,V,V,V,V],out_specs=[V,V],
        compiler_params=pltpu.CompilerParams(vmem_limit_bytes=VM2*2**20),
    )(jnp.swapaxes(offs,2,3),live,ext,probe,meas,hi,lo)


VM1, VM3 = 4, 16


MESH = pl.DeviceIdType.MESH


def put(src, dst, send, recv, device):
    return pltpu.make_async_remote_copy(src_ref=src, dst_ref=dst, send_sem=send, recv_sem=recv, device_id=device, device_id_type=MESH)


def places():
    row, col = lax.axis_index("row"), lax.axis_index("col")
    rows, cols = lax.axis_size("row"), lax.axis_size("col")
    return row, col, ((row + rows - 1) % rows, col), ((row + 1) % rows, col), (row, (col + cols - 1) % cols), (row, (col + 1) % cols)


def greet(devices):
    barrier = pltpu.get_barrier_semaphore()
    for device in devices:
        pl.semaphore_signal(barrier, inc=1, device_id=device, device_id_type=MESH)
    return barrier


def halo_kernel(tile, probe, meas, th, tl, ext, probev, measv, thv, tlv, hop1, hop2, loc, snd, rcv):
    row, col, up, down, left, right = places()
    loads = []

    def load(src, dst):
        c = pltpu.make_async_copy(src, dst, loc.at[len(loads)])
        loads.append(c)
        c.start()

    barrier = greet((right, up, down))
    pl.semaphore_wait(barrier, 3)
    n = [0]
    sent = []

    def send(src, dst, device):
        k = n[0]
        n[0] += 1
        c = put(src, dst, snd.at[k], rcv.at[k], device)
        c.start()
        sent.append(c)
        return c

    def lanes(cb):
        return pl.ds(128 * cb, 128)

    H = W // 2
    low = pl.ds(T, W)
    far = [pl.ds(T + H * k, H) for k in range(2)]
    first = [send(tile.at[:, pl.ds(H * k, H), lanes(3)], hop1.at[k], down) for k in range(2)]
    b = [send(tile.at[:, pl.ds(0, W), lanes(cb)], ext.at[:, cb, low, :], up) for cb in range(2)]
    r = [send(tile.at[:, :, lanes(cb)], ext.at[:, 4 + cb, pl.ds(0, T), :], left) for cb in range(2)]
    b2 = send(tile.at[:, pl.ds(0, W), lanes(2)], ext.at[:, 2, low, :], up)
    for cb in range(4):
        load(tile.at[:, :, lanes(cb)], ext.at[:, cb, pl.ds(0, T), :])
    for src, dst in ((probe, probev), (meas, measv), (th, thv), (tl, tlv)):
        load(src, dst)
    second, third, x = [], [], []
    for k in range(2):
        first[k].wait_recv()
        second.append(send(hop1.at[k], hop2.at[k], down))
    for k in range(2):
        b[k].wait_recv()
        x.append(send(ext.at[:, k, low, :], ext.at[:, 4 + k, low, :], left))
        second[k].wait_recv()
        third.append(send(hop2.at[k], ext.at[:, 3, far[k], :], down))
    for c in loads:
        c.wait()
    for c in (*r, b2, *third, *x):
        c.wait_recv()
    for c in sent:
        c.wait_send()


def halos(tile, probe, meas, th, tl):
    f = jnp.float32
    A = pl.BlockSpec(memory_space=pl.ANY)
    sd = jax.ShapeDtypeStruct
    H = W // 2
    same = [sd(a.shape, a.dtype) for a in (probe, meas, th, tl)]
    return pl.pallas_call(lambda *a: halo_kernel(*a), out_shape=[sd((2, 6, T + W, 128), f), *same],
        in_specs=[pl.BlockSpec(memory_space=pltpu.HBM)] * 5, out_specs=[A] * 5,
        scratch_shapes=[pltpu.VMEM((2, 2, H, 128), f), pltpu.VMEM((2, 2, H, 128), f), pltpu.SemaphoreType.DMA((8,)), pltpu.SemaphoreType.DMA((13,)), pltpu.SemaphoreType.DMA((13,))],
        compiler_params=pltpu.CompilerParams(collective_id=0, has_side_effects=True, vmem_limit_bytes=VM1*2**20))(tile, probe, meas, th, tl)


def spill_kernel(g, pg, grad, step, gv, rrv, brv, hop1, hop2, zhop1, zhop2, corner, bleft, mine, half, acc, plane, part, ybuf, shard, stepv, loc, snd, rcv, psnd, prcv, gsnd, grcv, zsnd, zrcv):
    row, col, up, down, left, right = places()
    rows, depth = lax.axis_size("row"), 4
    chips = lax.axis_size("col") // 2
    wide = chips // depth
    core, chip = col % 2, col // 2
    x, z = chip // depth, chip % depth
    H = W // 2
    step_rows = H // chips

    def at(xx, zz, cc):
        return (row, ((xx % wide) * depth + zz % depth) * 2 + cc)

    def peer(j):
        return (row, ((chip + j) % chips) * 2 + core)

    sib = at(x, z, 1 - core)
    zm = at(x, z + depth - 1, core)
    around = at(x + jnp.where(z == 1, 1, 0), z + depth - 1, 0)
    source = at(x + jnp.where(z == 0, wide - 1, 0), z + 1, 1)
    ys = [((row + k) % rows, col) for k in range(1, 4)]
    barrier = greet((left, sib, *ys))

    @pl.when(core == 0)
    def _():
        pl.semaphore_signal(barrier, inc=1, device_id=source, device_id_type=MESH)

    def hello(j, _):
        pl.semaphore_signal(barrier, inc=1, device_id=peer(j), device_id_type=MESH)
        return 0

    lax.fori_loop(1, chips, hello, 0)
    loads = []

    def load(src, dst):
        c = pltpu.make_async_copy(src, dst, loc.at[len(loads)])
        loads.append(c)
        c.start()
        return c

    def block(start, size):
        return pl.ds(pl.multiple_of(start, size), size)

    low, top = pl.ds(T, W), pl.ds(0, T)
    l_mine = load(pg.at[:, block(core * H, H), :], mine)
    l_left = load(g.at[:, pl.ds(0, 2), low, :], bleft)
    l_grad = load(g.at[:, pl.ds(0, 4), top, :], gv)
    pl.semaphore_wait(barrier, 5 + chips - 1 + core)
    n = [0]
    sent = []

    def send(src, dst, device):
        k = n[0]
        n[0] += 1
        c = put(src, dst, snd.at[k], rcv.at[k], device)
        c.start()
        sent.append(c)
        return c

    s1 = send(pg.at[:, block((1 - core) * H, H), :], half, sib)
    sc = [send(g.at[:, 4 + cb, low, :], corner.at[:, cb], right) for cb in range(2)]
    far = [pl.ds(H * k, H) for k in range(2)]
    first = [send(g.at[:, 3, pl.ds(T + H * k, H), :], hop1.at[k], up) for k in range(2)]
    b2 = send(g.at[:, 2, low, :], brv.at[:, 2], down)
    zrows = [pl.ds(H * (k + 1), H) for k in range(3)]

    def zcopy(level, k):
        if level == 0:
            return put(g.at[:, 5, zrows[k], :], zhop1.at[k], zsnd.at[k], zrcv.at[k], zm)
        if level == 1:
            return put(zhop1.at[k], zhop2.at[k], zsnd.at[3 + k], zrcv.at[3 + k], zm)
        return put(zhop2.at[k], rrv.at[:, 1, zrows[k], :], zsnd.at[6 + k], zrcv.at[6 + k], around)

    def zdirect(k):
        return put(g.at[:, 5, zrows[k], :], rrv.at[:, 1, zrows[k], :], zsnd.at[k], zrcv.at[6 + k], sib)

    @pl.when(core == 1)
    def _():
        for k in range(3):
            zcopy(0, k).start()

    @pl.when(core == 0)
    def _():
        for k in range(3):
            zdirect(k).start()

    l_mine.wait()
    s1.wait_recv()
    acc[...] = mine[...] + half[...]

    def shard_of(j):
        p = (chip + j) % chips
        return put(acc.at[:, block(p * step_rows, step_rows), :], plane.at[j], psnd.at[j], prcv.at[j], peer(j))

    def begin(j, _):
        shard_of(j).start()
        return 0

    lax.fori_loop(1, chips, begin, 0)
    r = [send(g.at[:, 4, top, :], rrv.at[:, 0], right), send(g.at[:, 5, pl.ds(0, H), :], rrv.at[:, 1, pl.ds(0, H), :], right)]
    l_left.wait()
    b, second, third = [], [], []
    for k in range(2):
        first[k].wait_recv()
        second.append(send(hop1.at[k], hop2.at[k], up))
    for cb in range(2):
        sc[cb].wait_recv()
        bleft[:, cb] += corner[:, cb]
        b.append(send(bleft.at[:, cb], brv.at[:, cb], down))

    @pl.when(core == 1)
    def _():
        for k in range(3):
            zcopy(0, k).wait_recv()
            zcopy(1, k).start()

    part[...] = acc[:, block(chip * step_rows, step_rows), :]

    def collect(j, _):
        shard_of(j).wait_recv()
        part[...] += plane[j]
        return 0

    lax.fori_loop(1, chips, collect, 0)
    yr = [send(part, ybuf.at[row], ys[k]) for k in range(3)]
    ybuf[pl.ds(row, 1)] = part[...][None]
    for k in range(2):
        second[k].wait_recv()
        third.append(send(hop2.at[k], brv.at[:, 3, far[k], :], up))

    @pl.when(core == 1)
    def _():
        for k in range(3):
            zcopy(1, k).wait_recv()
            zcopy(2, k).start()

    for c in yr:
        c.wait_recv()
    total = ybuf[0] + ybuf[1] + ybuf[2] + ybuf[3]
    shard[...] = total[:2] / jnp.sqrt(total[2:])
    here = block(core * H + chip * step_rows, step_rows)

    def gather(j):
        return put(shard, stepv.at[:, here, :], gsnd.at[j], grcv.at[j], peer(j))

    def begin2(j, _):
        gather(j).start()
        return 0

    lax.fori_loop(1, chips, begin2, 0)
    stepv[:, here, :] = shard[...]

    def collect2(j, _):
        gather(j).wait_recv()
        return 0

    lax.fori_loop(1, chips, collect2, 0)
    mine_rows = block(core * H, H)
    s5 = send(stepv.at[:, mine_rows, :], stepv.at[:, mine_rows, :], sib)
    l_grad.wait()
    for c in r:
        c.wait_recv()
    for k in range(3):
        zcopy(2, k).wait_recv()

    def add_left(k, _):
        at_rows = block(k * 32, 32)
        gv[:, :2, at_rows, :] += rrv[:, :, at_rows, :]
        return 0

    lax.fori_loop(0, T // 32, add_left, 0)
    for c in (b2, *b, *third):
        c.wait_recv()

    def add_top(k, _):
        at_rows = block(k * 32, 32)
        gv[:, :, at_rows, :] += brv[:, :, at_rows, :]
        return 0

    lax.fori_loop(0, W // 32, add_top, 0)
    outs = [load(gv.at[:, cb], grad.at[:, :, pl.ds(128 * cb, 128)]) for cb in range(4)]
    s5.wait_recv()
    outs.append(load(stepv, step))

    def drain(j, _):
        shard_of(j).wait_send()
        gather(j).wait_send()
        return 0

    lax.fori_loop(1, chips, drain, 0)
    for c in sent:
        c.wait_send()

    @pl.when(core == 1)
    def _():
        for level in range(3):
            for k in range(3):
                zcopy(level, k).wait_send()

    @pl.when(core == 0)
    def _():
        for k in range(3):
            zdirect(k).wait_send()

    for c in outs:
        c.wait()


def spills(g, pg, rows, cols):
    f = jnp.float32
    A = pl.BlockSpec(memory_space=pl.ANY)
    sd = jax.ShapeDtypeStruct
    V = pltpu.VMEM
    D = pltpu.SemaphoreType.DMA
    H = W // 2
    chips = cols // 2
    sh = H // chips
    return pl.pallas_call(lambda *a: spill_kernel(*a), out_shape=[sd((2, T, T), f), sd((2, W, W), f)],
        in_specs=[A] * 2, out_specs=[A, A],
        scratch_shapes=[V((2, 4, T, 128), f), V((2, 2, T, 128), f), V((2, 4, W, 128), f), V((2, 2, H, 128), f), V((2, 2, H, 128), f),
            V((3, 2, H, 128), f), V((3, 2, H, 128), f), V((2, 2, W, 128), f), V((2, 2, W, 128), f),
            V((3, H, W), f), V((3, H, W), f), V((3, H, W), f), V((chips, 3, sh, W), f), V((3, sh, W), f), V((rows, 3, sh, W), f), V((2, sh, W), f), V((2, W, W), f),
            D((8,)), D((18,)), D((18,)), D((chips,)), D((chips,)), D((chips,)), D((chips,)), D((9,)), D((9,))],
        compiler_params=pltpu.CompilerParams(collective_id=1, has_side_effects=True, vmem_limit_bytes=VM3*2**20))(g, pg)


def local(specimen, probe_field, measured, offsets, live_counts):
    hi, lo = tables()
    ext, probe, meas, hi, lo = halos(specimen, probe_field, measured[0, 0], jnp.asarray(hi), jnp.asarray(lo))
    g, pg = compute(offsets, live_counts, ext, probe, meas, hi, lo)
    grad, step = spills(g, pg, lax.axis_size("row"), lax.axis_size("col"))
    return (grad, step)


def solution(mesh):
    from jax.sharding import PartitionSpec as P
    in_specs = (P(None, "row", "col"), P(), P("row", "col", None, None, None), P("row", "col", None, None), P("row", "col"))
    out_specs = (P(None, "row", "col"), P())
    return jax.shard_map(local, mesh=mesh, in_specs=in_specs, out_specs=out_specs, check_vma=False)
```

```python
import functools, math
import jax, jax.numpy as jnp, numpy as np, ml_dtypes
from jax import lax
from jax.experimental import pallas as pl
from jax.experimental.pallas import tpu as pltpu

W=256; T=512; S=8
VM2=24
BF=jnp.bfloat16
def tables():
    k=np.arange(W); k=np.where(k<W//2,k,k-W).astype(np.float64)
    h=np.exp(-1j*math.pi*0.25*k*k/W)
    a=np.fft.ifft(h)
    H=W//2
    d=(np.arange(H)[:,None]-np.arange(H)[None,:])
    out=[]
    for sgn in (1,-1):
        c=0.5*(a[d%W]+sgn*a[(d+H)%W])
        ml=np.block([[c.real,-c.imag],[c.imag,c.real]])
        out.append(ml)
    ml=np.stack(out)
    mr=np.swapaxes(ml,1,2)
    def split(m):
        hi=m.astype(np.float32).astype(ml_dtypes.bfloat16)
        lo=(m-hi.astype(np.float64)).astype(np.float32).astype(ml_dtypes.bfloat16)
        return hi,lo
    lh,ll=split(ml); rh,rl=split(mr)
    return np.stack([lh,rh]),np.stack([ll,rl])

def split(x):
    hi=x.astype(BF)
    lo=(x-hi.astype(jnp.float32)).astype(BF)
    return hi,lo

def right_mul(xr,xi,th,tl,which):
    H=W//2
    outs=[]
    for n,(r,i) in enumerate(((xr[:,:H]+xr[:,H:],xi[:,:H]+xi[:,H:]),(xr[:,:H]-xr[:,H:],xi[:,:H]-xi[:,H:]))):
        s=jnp.concatenate([r,i],axis=1)
        hi,lo=split(s)
        lhs=jnp.concatenate([hi,hi,lo],axis=1)
        outs.append(jnp.dot(lhs,jnp.concatenate([th[1-which,n],tl[1-which,n],th[1-which,n]],axis=0),preferred_element_type=jnp.float32))
    u,v=outs
    yr=jnp.concatenate([u[:,:H]+v[:,:H],u[:,:H]-v[:,:H]],axis=1)
    yi=jnp.concatenate([u[:,H:]+v[:,H:],u[:,H:]-v[:,H:]],axis=1)
    return yr,yi

def left_mul(xr,xi,th,tl,which):
    H=W//2
    outs=[]
    for n,(r,i) in enumerate(((xr[:H]+xr[H:],xi[:H]+xi[H:]),(xr[:H]-xr[H:],xi[:H]-xi[H:]))):
        s=jnp.concatenate([r,i],axis=0)
        hi,lo=split(s)
        rhs=jnp.concatenate([hi,lo,hi],axis=0)
        outs.append(jnp.dot(jnp.concatenate([th[which,n],th[which,n],tl[which,n]],axis=1),rhs,preferred_element_type=jnp.float32))
    u,v=outs
    yr=jnp.concatenate([u[:H]+v[:H],u[:H]-v[:H]],axis=0)
    yi=jnp.concatenate([u[H:]+v[H:],u[H:]-v[H:]],axis=0)
    return yr,yi

def kernel(offs,live,ext,probe,mv,th,tl, grad,pg):
    grad[...]=jnp.zeros_like(grad)
    pg[...]=jnp.zeros_like(pg)
    lane=lax.broadcasted_iota(jnp.int32,(W,128),1)
    def slot(s,_):
        r0=offs[0,0,0,s]; c0=offs[0,0,1,s]
        q=c0//128; sh=c0-q*128
        keep=lane<128-sh
        o=[]
        for ch in range(2):
            x=[pltpu.roll(ext[ch,q+j,pl.ds(r0,W),:],128-sh,1) for j in range(3)]
            o.append(jnp.concatenate([jnp.where(keep,x[0],x[1]),jnp.where(keep,x[1],x[2])],axis=1))
        orr,oi=o
        pr=probe[0]; pi=probe[1]
        ar=pr*orr-pi*oi; ai=pr*oi+pi*orr
        ar,ai=right_mul(ar,ai,th,tl,0)
        ar,ai=left_mul(ar,ai,th,tl,0)
        res=ar*ar+ai*ai-mv[s]
        ar,ai=right_mul(res*ar,res*ai,th,tl,1)
        br,bi=left_mul(ar,ai,th,tl,1)
        pg[0]+=orr*br+oi*bi
        pg[1]+=orr*bi-oi*br
        pg[2]+=orr*orr+oi*oi
        gr=pr*br+pi*bi; gi=pr*bi-pi*br
        low=lane<sh
        for ch,g in enumerate((gr,gi)):
            a=pltpu.roll(g[:,:128],sh,1); b=pltpu.roll(g[:,128:],sh,1)
            z=jnp.zeros_like(a)
            grad[ch,q,pl.ds(r0,W),:]+=jnp.where(low,z,a)
            grad[ch,q+1,pl.ds(r0,W),:]+=jnp.where(low,a,b)
            grad[ch,q+2,pl.ds(r0,W),:]+=jnp.where(low,b,z)
        return 0
    lax.fori_loop(0,live[0,0],slot,0)


def compute(offs,live,ext,probe,meas,hi,lo):
    f=jnp.float32
    sd=jax.ShapeDtypeStruct
    V=pl.BlockSpec(memory_space=pltpu.VMEM); M=pl.BlockSpec(memory_space=pltpu.SMEM)
    return pl.pallas_call(kernel,
        out_shape=[sd((2,6,T+W,128),f),sd((3,W,W),f)],
        in_specs=[M,M,V,V,V,V,V],out_specs=[V,V],
        compiler_params=pltpu.CompilerParams(vmem_limit_bytes=VM2*2**20),
    )(jnp.swapaxes(offs,2,3),live,ext,probe,meas,hi,lo)


VM1, VM3 = 4, 16


MESH = pl.DeviceIdType.MESH


def put(src, dst, send, recv, device):
    return pltpu.make_async_remote_copy(src_ref=src, dst_ref=dst, send_sem=send, recv_sem=recv, device_id=device, device_id_type=MESH)


def places():
    row, col = lax.axis_index("row"), lax.axis_index("col")
    rows, cols = lax.axis_size("row"), lax.axis_size("col")
    return row, col, ((row + rows - 1) % rows, col), ((row + 1) % rows, col), (row, (col + cols - 1) % cols), (row, (col + 1) % cols)


def greet(devices):
    barrier = pltpu.get_barrier_semaphore()
    for device in devices:
        pl.semaphore_signal(barrier, inc=1, device_id=device, device_id_type=MESH)
    return barrier


def halo_kernel(tile, probe, meas, th, tl, ext, probev, measv, thv, tlv, hop1, hop2, loc, snd, rcv):
    row, col, up, down, left, right = places()
    loads = []

    def load(src, dst):
        c = pltpu.make_async_copy(src, dst, loc.at[len(loads)])
        loads.append(c)
        c.start()

    barrier = greet((right, up, down))
    pl.semaphore_wait(barrier, 3)
    n = [0]
    sent = []

    def send(src, dst, device):
        k = n[0]
        n[0] += 1
        c = put(src, dst, snd.at[k], rcv.at[k], device)
        c.start()
        sent.append(c)
        return c

    def lanes(cb):
        return pl.ds(128 * cb, 128)

    H = W // 2
    low = pl.ds(T, W)
    far = [pl.ds(T + H * k, H) for k in range(2)]
    first = [send(tile.at[:, pl.ds(H * k, H), lanes(3)], hop1.at[k], down) for k in range(2)]
    b = [send(tile.at[:, pl.ds(0, W), lanes(cb)], ext.at[:, cb, low, :], up) for cb in range(2)]
    r = [send(tile.at[:, :, lanes(cb)], ext.at[:, 4 + cb, pl.ds(0, T), :], left) for cb in range(2)]
    b2 = send(tile.at[:, pl.ds(0, W), lanes(2)], ext.at[:, 2, low, :], up)
    for cb in range(4):
        load(tile.at[:, :, lanes(cb)], ext.at[:, cb, pl.ds(0, T), :])
    for src, dst in ((probe, probev), (meas, measv), (th, thv), (tl, tlv)):
        load(src, dst)
    second, third, x = [], [], []
    for k in range(2):
        first[k].wait_recv()
        second.append(send(hop1.at[k], hop2.at[k], down))
    for k in range(2):
        b[k].wait_recv()
        x.append(send(ext.at[:, k, low, :], ext.at[:, 4 + k, low, :], left))
        second[k].wait_recv()
        third.append(send(hop2.at[k], ext.at[:, 3, far[k], :], down))
    for c in loads:
        c.wait()
    for c in (*r, b2, *third, *x):
        c.wait_recv()
    for c in sent:
        c.wait_send()


def halos(tile, probe, meas, th, tl):
    f = jnp.float32
    A = pl.BlockSpec(memory_space=pl.ANY)
    sd = jax.ShapeDtypeStruct
    H = W // 2
    same = [sd(a.shape, a.dtype) for a in (probe, meas, th, tl)]
    return pl.pallas_call(lambda *a: halo_kernel(*a), out_shape=[sd((2, 6, T + W, 128), f), *same],
        in_specs=[pl.BlockSpec(memory_space=pltpu.HBM)] * 5, out_specs=[A] * 5,
        scratch_shapes=[pltpu.VMEM((2, 2, H, 128), f), pltpu.VMEM((2, 2, H, 128), f), pltpu.SemaphoreType.DMA((8,)), pltpu.SemaphoreType.DMA((13,)), pltpu.SemaphoreType.DMA((13,))],
        compiler_params=pltpu.CompilerParams(collective_id=0, has_side_effects=True, vmem_limit_bytes=VM1*2**20))(*[pltpu.with_memory_space_constraint(a, pltpu.HBM) for a in (tile, probe, meas, th, tl)])


def spill_kernel(g, pg, grad, step, gv, rrv, brv, hop1, hop2, zhop1, zhop2, corner, bleft, mine, half, acc, plane, part, ybuf, shard, stepv, loc, snd, rcv, psnd, prcv, gsnd, grcv, zsnd, zrcv):
    row, col, up, down, left, right = places()
    rows, depth = lax.axis_size("row"), 4
    chips = lax.axis_size("col") // 2
    wide = chips // depth
    core, chip = col % 2, col // 2
    x, z = chip // depth, chip % depth
    H = W // 2
    step_rows = H // chips

    def at(xx, zz, cc):
        return (row, ((xx % wide) * depth + zz % depth) * 2 + cc)

    def peer(j):
        return (row, ((chip + j) % chips) * 2 + core)

    sib = at(x, z, 1 - core)
    zm = at(x, z + depth - 1, core)
    around = at(x + jnp.where(z == 1, 1, 0), z + depth - 1, 0)
    source = at(x + jnp.where(z == 0, wide - 1, 0), z + 1, 1)
    ys = [((row + k) % rows, col) for k in range(1, 4)]
    barrier = greet((left, sib, *ys))

    @pl.when(core == 0)
    def _():
        pl.semaphore_signal(barrier, inc=1, device_id=source, device_id_type=MESH)

    def hello(j, _):
        pl.semaphore_signal(barrier, inc=1, device_id=peer(j), device_id_type=MESH)
        return 0

    lax.fori_loop(1, chips, hello, 0)
    loads = []

    def load(src, dst):
        c = pltpu.make_async_copy(src, dst, loc.at[len(loads)])
        loads.append(c)
        c.start()
        return c

    def block(start, size):
        return pl.ds(pl.multiple_of(start, size), size)

    low, top = pl.ds(T, W), pl.ds(0, T)
    l_mine = load(pg.at[:, block(core * H, H), :], mine)
    l_left = load(g.at[:, pl.ds(0, 2), low, :], bleft)
    l_grad = load(g.at[:, pl.ds(0, 4), top, :], gv)
    pl.semaphore_wait(barrier, 5 + chips - 1 + core)
    n = [0]
    sent = []

    def send(src, dst, device):
        k = n[0]
        n[0] += 1
        c = put(src, dst, snd.at[k], rcv.at[k], device)
        c.start()
        sent.append(c)
        return c

    s1 = send(pg.at[:, block((1 - core) * H, H), :], half, sib)
    sc = [send(g.at[:, 4 + cb, low, :], corner.at[:, cb], right) for cb in range(2)]
    far = [pl.ds(H * k, H) for k in range(2)]
    first = [send(g.at[:, 3, pl.ds(T + H * k, H), :], hop1.at[k], up) for k in range(2)]
    b2 = send(g.at[:, 2, low, :], brv.at[:, 2], down)
    zrows = [pl.ds(H * (k + 1), H) for k in range(3)]

    def zcopy(level, k):
        if level == 0:
            return put(g.at[:, 5, zrows[k], :], zhop1.at[k], zsnd.at[k], zrcv.at[k], zm)
        if level == 1:
            return put(zhop1.at[k], zhop2.at[k], zsnd.at[3 + k], zrcv.at[3 + k], zm)
        return put(zhop2.at[k], rrv.at[:, 1, zrows[k], :], zsnd.at[6 + k], zrcv.at[6 + k], around)

    def zdirect(k):
        return put(g.at[:, 5, zrows[k], :], rrv.at[:, 1, zrows[k], :], zsnd.at[k], zrcv.at[6 + k], sib)

    @pl.when(core == 1)
    def _():
        for k in range(3):
            zcopy(0, k).start()

    @pl.when(core == 0)
    def _():
        for k in range(3):
            zdirect(k).start()

    l_mine.wait()
    s1.wait_recv()
    acc[...] = mine[...] + half[...]

    def shard_of(j):
        p = (chip + j) % chips
        return put(acc.at[:, block(p * step_rows, step_rows), :], plane.at[j], psnd.at[j], prcv.at[j], peer(j))

    def begin(j, _):
        shard_of(j).start()
        return 0

    lax.fori_loop(1, chips, begin, 0)
    r = [send(g.at[:, 4, top, :], rrv.at[:, 0], right), send(g.at[:, 5, pl.ds(0, H), :], rrv.at[:, 1, pl.ds(0, H), :], right)]
    l_left.wait()
    b, second, third = [], [], []
    for k in range(2):
        first[k].wait_recv()
        second.append(send(hop1.at[k], hop2.at[k], up))
    for cb in range(2):
        sc[cb].wait_recv()
        bleft[:, cb] += corner[:, cb]
        b.append(send(bleft.at[:, cb], brv.at[:, cb], down))

    @pl.when(core == 1)
    def _():
        for k in range(3):
            zcopy(0, k).wait_recv()
            zcopy(1, k).start()

    part[...] = acc[:, block(chip * step_rows, step_rows), :]

    def collect(j, _):
        shard_of(j).wait_recv()
        part[...] += plane[j]
        return 0

    lax.fori_loop(1, chips, collect, 0)
    yr = [send(part, ybuf.at[row], ys[k]) for k in range(3)]
    ybuf[pl.ds(row, 1)] = part[...][None]
    for k in range(2):
        second[k].wait_recv()
        third.append(send(hop2.at[k], brv.at[:, 3, far[k], :], up))

    @pl.when(core == 1)
    def _():
        for k in range(3):
            zcopy(1, k).wait_recv()
            zcopy(2, k).start()

    for c in yr:
        c.wait_recv()
    total = ybuf[0] + ybuf[1] + ybuf[2] + ybuf[3]
    shard[...] = total[:2] / jnp.sqrt(total[2:])
    here = block(core * H + chip * step_rows, step_rows)

    def gather(j):
        return put(shard, stepv.at[:, here, :], gsnd.at[j], grcv.at[j], peer(j))

    def begin2(j, _):
        gather(j).start()
        return 0

    lax.fori_loop(1, chips, begin2, 0)
    stepv[:, here, :] = shard[...]

    def collect2(j, _):
        gather(j).wait_recv()
        return 0

    lax.fori_loop(1, chips, collect2, 0)
    mine_rows = block(core * H, H)
    s5 = send(stepv.at[:, mine_rows, :], stepv.at[:, mine_rows, :], sib)
    l_grad.wait()
    for c in r:
        c.wait_recv()
    for k in range(3):
        zcopy(2, k).wait_recv()

    def add_left(k, _):
        at_rows = block(k * 32, 32)
        gv[:, :2, at_rows, :] += rrv[:, :, at_rows, :]
        return 0

    lax.fori_loop(0, T // 32, add_left, 0)
    for c in (b2, *b, *third):
        c.wait_recv()

    def add_top(k, _):
        at_rows = block(k * 32, 32)
        gv[:, :, at_rows, :] += brv[:, :, at_rows, :]
        return 0

    lax.fori_loop(0, W // 32, add_top, 0)
    outs = [load(gv.at[:, cb], grad.at[:, :, pl.ds(128 * cb, 128)]) for cb in range(4)]
    s5.wait_recv()
    outs.append(load(stepv, step))

    def drain(j, _):
        shard_of(j).wait_send()
        gather(j).wait_send()
        return 0

    lax.fori_loop(1, chips, drain, 0)
    for c in sent:
        c.wait_send()

    @pl.when(core == 1)
    def _():
        for level in range(3):
            for k in range(3):
                zcopy(level, k).wait_send()

    @pl.when(core == 0)
    def _():
        for k in range(3):
            zdirect(k).wait_send()

    for c in outs:
        c.wait()


def spills(g, pg, rows, cols):
    f = jnp.float32
    A = pl.BlockSpec(memory_space=pl.ANY)
    sd = jax.ShapeDtypeStruct
    V = pltpu.VMEM
    D = pltpu.SemaphoreType.DMA
    H = W // 2
    chips = cols // 2
    sh = H // chips
    return pl.pallas_call(lambda *a: spill_kernel(*a), out_shape=[sd((2, T, T), f), sd((2, W, W), f)],
        in_specs=[A] * 2, out_specs=[A, A],
        scratch_shapes=[V((2, 4, T, 128), f), V((2, 2, T, 128), f), V((2, 4, W, 128), f), V((2, 2, H, 128), f), V((2, 2, H, 128), f),
            V((3, 2, H, 128), f), V((3, 2, H, 128), f), V((2, 2, W, 128), f), V((2, 2, W, 128), f),
            V((3, H, W), f), V((3, H, W), f), V((3, H, W), f), V((chips, 3, sh, W), f), V((3, sh, W), f), V((rows, 3, sh, W), f), V((2, sh, W), f), V((2, W, W), f),
            D((8,)), D((18,)), D((18,)), D((chips,)), D((chips,)), D((chips,)), D((chips,)), D((9,)), D((9,))],
        compiler_params=pltpu.CompilerParams(collective_id=1, has_side_effects=True, vmem_limit_bytes=VM3*2**20))(g, pg)


def local(specimen, probe_field, measured, offsets, live_counts):
    hi, lo = tables()
    ext, probe, meas, hi, lo = halos(specimen, probe_field, measured[0, 0], jnp.asarray(hi), jnp.asarray(lo))
    g, pg = compute(offsets, live_counts, ext, probe, meas, hi, lo)
    grad, step = spills(g, pg, lax.axis_size("row"), lax.axis_size("col"))
    return (grad, step)


def solution(mesh):
    from jax.sharding import PartitionSpec as P
    in_specs = (P(None, "row", "col"), P(), P("row", "col", None, None, None), P("row", "col", None, None), P("row", "col"))
    out_specs = (P(None, "row", "col"), P())
    return jax.shard_map(local, mesh=mesh, in_specs=in_specs, out_specs=out_specs, check_vma=False)
```

```python
import functools, math
import jax, jax.numpy as jnp, numpy as np, ml_dtypes
from jax import lax
from jax.experimental import pallas as pl
from jax.experimental.pallas import tpu as pltpu

W=256; T=512; S=8
VM2=24
BF=jnp.bfloat16
def tables():
    k=np.arange(W); k=np.where(k<W//2,k,k-W).astype(np.float64)
    h=np.exp(-1j*math.pi*0.25*k*k/W)
    a=np.fft.ifft(h)
    H=W//2
    d=(np.arange(H)[:,None]-np.arange(H)[None,:])
    out=[]
    for sgn in (1,-1):
        c=0.5*(a[d%W]+sgn*a[(d+H)%W])
        ml=np.block([[c.real,-c.imag],[c.imag,c.real]])
        out.append(ml)
    ml=np.stack(out)
    mr=np.swapaxes(ml,1,2)
    def split(m):
        hi=m.astype(np.float32).astype(ml_dtypes.bfloat16)
        lo=(m-hi.astype(np.float64)).astype(np.float32).astype(ml_dtypes.bfloat16)
        return hi,lo
    lh,ll=split(ml); rh,rl=split(mr)
    return np.stack([lh,rh]),np.stack([ll,rl])

def split(x):
    hi=x.astype(BF)
    lo=(x-hi.astype(jnp.float32)).astype(BF)
    return hi,lo

def right_mul(xr,xi,th,tl,which):
    H=W//2
    outs=[]
    for n,(r,i) in enumerate(((xr[:,:H]+xr[:,H:],xi[:,:H]+xi[:,H:]),(xr[:,:H]-xr[:,H:],xi[:,:H]-xi[:,H:]))):
        s=jnp.concatenate([r,i],axis=1)
        hi,lo=split(s)
        lhs=jnp.concatenate([hi,hi,lo],axis=1)
        outs.append(jnp.dot(lhs,jnp.concatenate([th[1-which,n],tl[1-which,n],th[1-which,n]],axis=0),preferred_element_type=jnp.float32))
    u,v=outs
    yr=jnp.concatenate([u[:,:H]+v[:,:H],u[:,:H]-v[:,:H]],axis=1)
    yi=jnp.concatenate([u[:,H:]+v[:,H:],u[:,H:]-v[:,H:]],axis=1)
    return yr,yi

def left_mul(xr,xi,th,tl,which):
    H=W//2
    outs=[]
    for n,(r,i) in enumerate(((xr[:H]+xr[H:],xi[:H]+xi[H:]),(xr[:H]-xr[H:],xi[:H]-xi[H:]))):
        s=jnp.concatenate([r,i],axis=0)
        hi,lo=split(s)
        rhs=jnp.concatenate([hi,lo,hi],axis=0)
        outs.append(jnp.dot(jnp.concatenate([th[which,n],th[which,n],tl[which,n]],axis=1),rhs,preferred_element_type=jnp.float32))
    u,v=outs
    yr=jnp.concatenate([u[:H]+v[:H],u[:H]-v[:H]],axis=0)
    yi=jnp.concatenate([u[H:]+v[H:],u[H:]-v[H:]],axis=0)
    return yr,yi

def kernel(offs,live,ext,probe,mv,th,tl, grad,pg):
    grad[...]=jnp.zeros_like(grad)
    pg[...]=jnp.zeros_like(pg)
    lane=lax.broadcasted_iota(jnp.int32,(W,128),1)
    def open_slot(s,on):
        r0=offs[0,0,0,s]; c0=offs[0,0,1,s]
        q=c0//128; sh=c0-q*128
        keep=lane<128-sh
        o=[]
        for ch in range(2):
            x=[pltpu.roll(ext[ch,q+j,pl.ds(r0,W),:],128-sh,1) for j in range(3)]
            o.append(jnp.concatenate([jnp.where(keep,x[0],x[1]),jnp.where(keep,x[1],x[2])],axis=1))
        orr,oi=o
        pr=probe[0]; pi=probe[1]
        return (s,on,r0,q,sh,orr,oi),(pr*orr-pi*oi,pr*oi+pi*orr)
    def middle(st,a):
        ar,ai=a
        s,on=st[:2]
        res=(ar*ar+ai*ai-mv[s])
        if on is not None: res=res*on
        return res*ar,res*ai
    def close_slot(st,a):
        s,on,r0,q,sh,orr,oi=st
        br,bi=a
        pr=probe[0]; pi=probe[1]
        pg[0]+=orr*br+oi*bi
        pg[1]+=orr*bi-oi*br
        il=orr*orr+oi*oi
        pg[2]+=il if on is None else il*on
        gr=pr*br+pi*bi; gi=pr*bi-pi*br
        low=lane<sh
        for ch,g in enumerate((gr,gi)):
            a=pltpu.roll(g[:,:128],sh,1); b=pltpu.roll(g[:,128:],sh,1)
            z=jnp.zeros_like(a)
            grad[ch,q,pl.ds(r0,W),:]+=jnp.where(low,z,a)
            grad[ch,q+1,pl.ds(r0,W),:]+=jnp.where(low,a,b)
            grad[ch,q+2,pl.ds(r0,W),:]+=jnp.where(low,b,z)
    def pair(p,_):
        on=(2*p+1<live[0,0]).astype(jnp.float32)
        sts,vs=zip(*[open_slot(2*p,None),open_slot(2*p+1,on)])
        vs=[right_mul(*v,th,tl,0) for v in vs]
        vs=[left_mul(*v,th,tl,0) for v in vs]
        vs=[middle(st,v) for st,v in zip(sts,vs)]
        vs=[right_mul(*v,th,tl,1) for v in vs]
        vs=[left_mul(*v,th,tl,1) for v in vs]
        for st,v in zip(sts,vs): close_slot(st,v)
        return 0
    lax.fori_loop(0,(live[0,0]+1)//2,pair,0)

def compute(offs,live,ext,probe,meas,hi,lo):
    f=jnp.float32
    sd=jax.ShapeDtypeStruct
    V=pl.BlockSpec(memory_space=pltpu.VMEM); M=pl.BlockSpec(memory_space=pltpu.SMEM)
    return pl.pallas_call(kernel,
        out_shape=[sd((2,6,T+W,128),f),sd((3,W,W),f)],
        in_specs=[M,M,V,V,V,V,V],out_specs=[V,V],
        compiler_params=pltpu.CompilerParams(vmem_limit_bytes=VM2*2**20),
    )(jnp.swapaxes(offs,2,3),live,ext,probe,meas,hi,lo)


VM1, VM3, NC = 4, 16, 64


MESH = pl.DeviceIdType.MESH


def put(src, dst, send, recv, device):
    return pltpu.make_async_remote_copy(src_ref=src, dst_ref=dst, send_sem=send, recv_sem=recv, device_id=device, device_id_type=MESH)


def places():
    row, col = lax.axis_index("row"), lax.axis_index("col")
    rows, cols = lax.axis_size("row"), lax.axis_size("col")
    return row, col, ((row + rows - 1) % rows, col), ((row + 1) % rows, col), (row, (col + cols - 1) % cols), (row, (col + 1) % cols)


def greet(devices):
    barrier = pltpu.get_barrier_semaphore()
    for device in devices:
        pl.semaphore_signal(barrier, inc=1, device_id=device, device_id_type=MESH)
    return barrier


def halo_kernel(tile, probe, meas, th, tl, ext, probev, measv, thv, tlv, hop1, hop2, loc, snd, rcv):
    row, col, up, down, left, right = places()
    loads = []

    def load(src, dst):
        c = pltpu.make_async_copy(src, dst, loc.at[len(loads)])
        loads.append(c)
        c.start()

    barrier = greet((right, up, down))
    pl.semaphore_wait(barrier, 3)
    n = [0]
    sent = []

    def send(src, dst, device):
        k = n[0]
        n[0] += 1
        c = put(src, dst, snd.at[k], rcv.at[k], device)
        c.start()
        sent.append(c)
        return c

    def lanes(cb):
        return pl.ds(128 * cb, 128)

    H = W // 2
    low = pl.ds(T, W)
    far = [pl.ds(T + H * k, H) for k in range(2)]
    first = [send(tile.at[:, pl.ds(H * k, H), lanes(3)], hop1.at[k], down) for k in range(2)]
    b = [send(tile.at[:, pl.ds(0, W), lanes(cb)], ext.at[:, cb, low, :], up) for cb in range(2)]
    r = [send(tile.at[:, :, lanes(cb)], ext.at[:, 4 + cb, pl.ds(0, T), :], left) for cb in range(2)]
    b2 = send(tile.at[:, pl.ds(0, W), lanes(2)], ext.at[:, 2, low, :], up)
    for cb in range(4):
        load(tile.at[:, :, lanes(cb)], ext.at[:, cb, pl.ds(0, T), :])
    for src, dst in ((probe, probev), (meas, measv), (th, thv), (tl, tlv)):
        load(src, dst)
    second, third, x = [], [], []
    for k in range(2):
        first[k].wait_recv()
        second.append(send(hop1.at[k], hop2.at[k], down))
    for k in range(2):
        b[k].wait_recv()
        x.append(send(ext.at[:, k, low, :], ext.at[:, 4 + k, low, :], left))
        second[k].wait_recv()
        third.append(send(hop2.at[k], ext.at[:, 3, far[k], :], down))
    for c in loads:
        c.wait()
    for c in (*r, b2, *third, *x):
        c.wait_recv()
    for c in sent:
        c.wait_send()


def halos(tile, probe, meas, th, tl):
    f = jnp.float32
    A = pl.BlockSpec(memory_space=pl.ANY)
    sd = jax.ShapeDtypeStruct
    H = W // 2
    same = [sd(a.shape, a.dtype) for a in (probe, meas, th, tl)]
    return pl.pallas_call(lambda *a: halo_kernel(*a), out_shape=[sd((2, 6, T + W, 128), f), *same],
        in_specs=[pl.BlockSpec(memory_space=pltpu.HBM)] * 5, out_specs=[A] * 5,
        scratch_shapes=[pltpu.VMEM((2, 2, H, 128), f), pltpu.VMEM((2, 2, H, 128), f), pltpu.SemaphoreType.DMA((8,)), pltpu.SemaphoreType.DMA((13,)), pltpu.SemaphoreType.DMA((13,))],
        compiler_params=pltpu.CompilerParams(collective_id=0, has_side_effects=True, vmem_limit_bytes=VM1*2**20))(*[pltpu.with_memory_space_constraint(a, pltpu.HBM) for a in (tile, probe, meas, th, tl)])


GIVE = ((0, 1), (2,), (3,))


def spill_kernel(g, pg, grad, step, gv, rrv, brv, hop1, hop2, zhop1, zhop2, corner, bleft, mine, half, acc, plane, part, ybuf, shard, stepv, loc, snd, rcv, psnd, prcv, gsnd, grcv, zsnd, zrcv):
    row, col, up, down, left, right = places()
    rows, depth = lax.axis_size("row"), 4
    chips = lax.axis_size("col") // 2
    wide = chips // depth
    core, chip = col % 2, col // 2
    x, z = chip // depth, chip % depth
    H = W // 2
    step_rows = H // chips

    def at(xx, zz, cc):
        return (row, ((xx % wide) * depth + zz % depth) * 2 + cc)

    def peer(j):
        return (row, ((chip + j) % chips) * 2 + core)

    sib = at(x, z, 1 - core)
    zm = at(x, z + depth - 1, core)
    around = at(x + jnp.where(z == 1, 1, 0), z + depth - 1, 0)
    source = at(x + jnp.where(z == 0, wide - 1, 0), z + 1, 1)
    ys = [((row + k) % rows, col) for k in range(1, 4)]
    barrier = greet((left, sib, *ys))

    @pl.when(core == 0)
    def _():
        pl.semaphore_signal(barrier, inc=1, device_id=source, device_id_type=MESH)

    def hello(j, _):
        pl.semaphore_signal(barrier, inc=1, device_id=peer(j), device_id_type=MESH)
        return 0

    lax.fori_loop(1, chips, hello, 0)
    loads = []

    def load(src, dst):
        c = pltpu.make_async_copy(src, dst, loc.at[len(loads)])
        loads.append(c)
        c.start()
        return c

    def block(start, size):
        return pl.ds(pl.multiple_of(start, size), size)

    low, top = pl.ds(T, W), pl.ds(0, T)
    l_mine = load(pg.at[:, block(core * H, H), :], mine)
    l_left = load(g.at[:, pl.ds(0, 2), low, :], bleft)
    l_grad = load(g.at[:, pl.ds(0, 4), top, :], gv)
    pl.semaphore_wait(barrier, 5 + chips - 1 + core)
    n = [0]
    sent = []

    def send(src, dst, device):
        k = n[0]
        n[0] += 1
        c = put(src, dst, snd.at[k], rcv.at[k], device)
        c.start()
        sent.append(c)
        return c

    s1 = send(pg.at[:, block((1 - core) * H, H), :], half, sib)
    cuts = [pl.ds(NC * k, NC) for k in range(W // NC)]
    sc = [send(g.at[:, 4:6, pl.ds(T + NC * k, NC), :], corner.at[:, :, cuts[k], :], right) for k in range(W // NC)]
    far = [pl.ds(H * k, H) for k in range(2)]
    first = [send(g.at[:, 3, pl.ds(T + H * k, H), :], hop1.at[k], up) for k in range(2)]
    b2 = send(g.at[:, 2, low, :], brv.at[:, 2], down)
    zrows = [pl.ds(H * (k + 1), H) for k in range(3)]

    def zcopy(level, k):
        if level == 0:
            return put(g.at[:, 5, zrows[k], :], zhop1.at[k], zsnd.at[k], zrcv.at[k], zm)
        if level == 1:
            return put(zhop1.at[k], zhop2.at[k], zsnd.at[3 + k], zrcv.at[3 + k], zm)
        return put(zhop2.at[k], rrv.at[:, 1, zrows[k], :], zsnd.at[6 + k], zrcv.at[6 + k], around)

    def zdirect(k):
        return put(g.at[:, 5, zrows[k], :], rrv.at[:, 1, zrows[k], :], zsnd.at[k], zrcv.at[6 + k], sib)

    @pl.when(core == 1)
    def _():
        for k in range(3):
            zcopy(0, k).start()

    @pl.when(core == 0)
    def _():
        for k in range(3):
            zdirect(k).start()

    l_mine.wait()
    s1.wait_recv()
    acc[...] = mine[...] + half[...]

    def shard_of(j):
        p = (chip + j) % chips
        return put(acc.at[:, block(p * step_rows, step_rows), :], plane.at[j], psnd.at[j], prcv.at[j], peer(j))

    def begin(j, _):
        shard_of(j).start()
        return 0

    lax.fori_loop(1, chips, begin, 0)
    r = [send(g.at[:, 4, top, :], rrv.at[:, 0], right), send(g.at[:, 5, pl.ds(0, H), :], rrv.at[:, 1, pl.ds(0, H), :], right)]
    l_left.wait()
    b, second, third = [], [], []
    def give(k):
        sc[k].wait_recv()
        bleft[:, :, cuts[k], :] += corner[:, :, cuts[k], :]
        b.append(send(bleft.at[:, :, cuts[k], :], brv.at[:, 0:2, cuts[k], :], down))

    for k in GIVE[0]:
        give(k)
    for j in range(2):
        first[j].wait_recv()
        second.append(send(hop1.at[j], hop2.at[j], up))

    @pl.when(core == 1)
    def _():
        for k in range(3):
            zcopy(0, k).wait_recv()
            zcopy(1, k).start()

    part[...] = acc[:, block(chip * step_rows, step_rows), :]

    def collect(j, _):
        shard_of(j).wait_recv()
        part[...] += plane[j]
        return 0

    lax.fori_loop(1, chips, collect, 0)
    yr = [send(part, ybuf.at[row], ys[k]) for k in range(3)]
    ybuf[pl.ds(row, 1)] = part[...][None]
    for k in GIVE[1]:
        give(k)
    for c in yr:
        c.wait_recv()
    total = ybuf[0] + ybuf[1] + ybuf[2] + ybuf[3]
    shard[...] = total[:2] / jnp.sqrt(total[2:])
    here = block(core * H + chip * step_rows, step_rows)

    def gather(j):
        return put(shard, stepv.at[:, here, :], gsnd.at[j], grcv.at[j], peer(j))

    def begin2(j, _):
        gather(j).start()
        return 0

    lax.fori_loop(1, chips, begin2, 0)
    stepv[:, here, :] = shard[...]
    for k in GIVE[2]:
        give(k)
    for k in range(2):
        second[k].wait_recv()
        third.append(send(hop2.at[k], brv.at[:, 3, far[k], :], up))

    @pl.when(core == 1)
    def _():
        for k in range(3):
            zcopy(1, k).wait_recv()
            zcopy(2, k).start()


    def collect2(j, _):
        gather(j).wait_recv()
        return 0

    lax.fori_loop(1, chips, collect2, 0)
    mine_rows = block(core * H, H)
    s5 = send(stepv.at[:, mine_rows, :], stepv.at[:, mine_rows, :], sib)
    l_grad.wait()
    for c in r:
        c.wait_recv()
    for k in range(3):
        zcopy(2, k).wait_recv()

    def add_left(k, _):
        at_rows = block(k * 32, 32)
        gv[:, :2, at_rows, :] += rrv[:, :, at_rows, :]
        return 0

    lax.fori_loop(0, T // 32, add_left, 0)
    for c in (b2, *b, *third):
        c.wait_recv()

    def add_top(k, _):
        at_rows = block(k * 32, 32)
        gv[:, :, at_rows, :] += brv[:, :, at_rows, :]
        return 0

    lax.fori_loop(0, W // 32, add_top, 0)
    outs = [load(gv.at[:, cb], grad.at[:, :, pl.ds(128 * cb, 128)]) for cb in range(4)]
    s5.wait_recv()
    outs.append(load(stepv, step))

    def drain(j, _):
        shard_of(j).wait_send()
        gather(j).wait_send()
        return 0

    lax.fori_loop(1, chips, drain, 0)
    for c in sent:
        c.wait_send()

    @pl.when(core == 1)
    def _():
        for level in range(3):
            for k in range(3):
                zcopy(level, k).wait_send()

    @pl.when(core == 0)
    def _():
        for k in range(3):
            zdirect(k).wait_send()

    for c in outs:
        c.wait()


def spills(g, pg, rows, cols):
    f = jnp.float32
    A = pl.BlockSpec(memory_space=pl.ANY)
    sd = jax.ShapeDtypeStruct
    V = pltpu.VMEM
    D = pltpu.SemaphoreType.DMA
    H = W // 2
    chips = cols // 2
    sh = H // chips
    return pl.pallas_call(lambda *a: spill_kernel(*a), out_shape=[sd((2, T, T), f), sd((2, W, W), f)],
        in_specs=[A] * 2, out_specs=[A, A],
        scratch_shapes=[V((2, 4, T, 128), f), V((2, 2, T, 128), f), V((2, 4, W, 128), f), V((2, 2, H, 128), f), V((2, 2, H, 128), f),
            V((3, 2, H, 128), f), V((3, 2, H, 128), f), V((2, 2, W, 128), f), V((2, 2, W, 128), f),
            V((3, H, W), f), V((3, H, W), f), V((3, H, W), f), V((chips, 3, sh, W), f), V((3, sh, W), f), V((rows, 3, sh, W), f), V((2, sh, W), f), V((2, W, W), f),
            D((8,)), D((40,)), D((40,)), D((chips,)), D((chips,)), D((chips,)), D((chips,)), D((9,)), D((9,))],
        compiler_params=pltpu.CompilerParams(collective_id=1, has_side_effects=True, vmem_limit_bytes=VM3*2**20))(g, pg)


def local(specimen, probe_field, measured, offsets, live_counts):
    hi, lo = tables()
    ext, probe, meas, hi, lo = halos(specimen, probe_field, measured[0, 0], jnp.asarray(hi), jnp.asarray(lo))
    g, pg = compute(offsets, live_counts, ext, probe, meas, hi, lo)
    grad, step = spills(g, pg, lax.axis_size("row"), lax.axis_size("col"))
    return (grad, step)


def solution(mesh):
    from jax.sharding import PartitionSpec as P
    in_specs = (P(None, "row", "col"), P(), P("row", "col", None, None, None), P("row", "col", None, None), P("row", "col"))
    out_specs = (P(None, "row", "col"), P())
    return jax.shard_map(local, mesh=mesh, in_specs=in_specs, out_specs=out_specs, check_vma=False)
```

```python
import functools, math
import jax, jax.numpy as jnp, numpy as np, ml_dtypes
from jax import lax
from jax.experimental import pallas as pl
from jax.experimental.pallas import tpu as pltpu

W=256; T=512; S=8
VM2=24
BF=jnp.bfloat16
def tables():
    k=np.arange(W); k=np.where(k<W//2,k,k-W).astype(np.float64)
    h=np.exp(-1j*math.pi*0.25*k*k/W)
    a=np.fft.ifft(h)
    H=W//2
    d=(np.arange(H)[:,None]-np.arange(H)[None,:])
    out=[]
    for sgn in (1,-1):
        c=0.5*(a[d%W]+sgn*a[(d+H)%W])
        ml=np.block([[c.real,-c.imag],[c.imag,c.real]])
        out.append(ml)
    ml=np.stack(out)
    mr=np.swapaxes(ml,1,2)
    def split(m):
        hi=m.astype(np.float32).astype(ml_dtypes.bfloat16)
        lo=(m-hi.astype(np.float64)).astype(np.float32).astype(ml_dtypes.bfloat16)
        return hi,lo
    lh,ll=split(ml); rh,rl=split(mr)
    return np.stack([lh,rh]),np.stack([ll,rl])

def split(x):
    hi=x.astype(BF)
    lo=(x-hi.astype(jnp.float32)).astype(BF)
    return hi,lo

def right_mul(xr,xi,th,tl,which):
    H=W//2
    outs=[]
    for n,(r,i) in enumerate(((xr[:,:H]+xr[:,H:],xi[:,:H]+xi[:,H:]),(xr[:,:H]-xr[:,H:],xi[:,:H]-xi[:,H:]))):
        s=jnp.concatenate([r,i],axis=1)
        hi,lo=split(s)
        lhs=jnp.concatenate([hi,hi,lo],axis=1)
        outs.append(jnp.dot(lhs,jnp.concatenate([th[1-which,n],tl[1-which,n],th[1-which,n]],axis=0),preferred_element_type=jnp.float32))
    u,v=outs
    yr=jnp.concatenate([u[:,:H]+v[:,:H],u[:,:H]-v[:,:H]],axis=1)
    yi=jnp.concatenate([u[:,H:]+v[:,H:],u[:,H:]-v[:,H:]],axis=1)
    return yr,yi

def left_mul(xr,xi,th,tl,which):
    H=W//2
    outs=[]
    for n,(r,i) in enumerate(((xr[:H]+xr[H:],xi[:H]+xi[H:]),(xr[:H]-xr[H:],xi[:H]-xi[H:]))):
        s=jnp.concatenate([r,i],axis=0)
        hi,lo=split(s)
        rhs=jnp.concatenate([hi,lo,hi],axis=0)
        outs.append(jnp.dot(jnp.concatenate([th[which,n],th[which,n],tl[which,n]],axis=1),rhs,preferred_element_type=jnp.float32))
    u,v=outs
    yr=jnp.concatenate([u[:H]+v[:H],u[:H]-v[:H]],axis=0)
    yi=jnp.concatenate([u[H:]+v[H:],u[H:]-v[H:]],axis=0)
    return yr,yi

def kernel(offs,live,ext,probe,mv,th,tl, grad,pg):
    grad[...]=jnp.zeros_like(grad)
    pg[...]=jnp.zeros_like(pg)
    lane=lax.broadcasted_iota(jnp.int32,(W,128),1)
    def open_slot(s,on):
        r0=offs[0,0,0,s]; c0=offs[0,0,1,s]
        q=c0//128; sh=c0-q*128
        keep=lane<128-sh
        o=[]
        for ch in range(2):
            x=[pltpu.roll(ext[ch,q+j,pl.ds(r0,W),:],128-sh,1) for j in range(3)]
            o.append(jnp.concatenate([jnp.where(keep,x[0],x[1]),jnp.where(keep,x[1],x[2])],axis=1))
        orr,oi=o
        pr=probe[0]; pi=probe[1]
        return (s,on,r0,q,sh,orr,oi),(pr*orr-pi*oi,pr*oi+pi*orr)
    def middle(st,a):
        ar,ai=a
        s,on=st[:2]
        res=(ar*ar+ai*ai-mv[s])
        if on is not None: res=res*on
        return res*ar,res*ai
    def close_slot(st,a):
        s,on,r0,q,sh,orr,oi=st
        br,bi=a
        pr=probe[0]; pi=probe[1]
        pg[0]+=orr*br+oi*bi
        pg[1]+=orr*bi-oi*br
        il=orr*orr+oi*oi
        pg[2]+=il if on is None else il*on
        gr=pr*br+pi*bi; gi=pr*bi-pi*br
        low=lane<sh
        for ch,g in enumerate((gr,gi)):
            a=pltpu.roll(g[:,:128],sh,1); b=pltpu.roll(g[:,128:],sh,1)
            z=jnp.zeros_like(a)
            grad[ch,q,pl.ds(r0,W),:]+=jnp.where(low,z,a)
            grad[ch,q+1,pl.ds(r0,W),:]+=jnp.where(low,a,b)
            grad[ch,q+2,pl.ds(r0,W),:]+=jnp.where(low,b,z)
    def pair(p,_):
        on=(2*p+1<live[0,0]).astype(jnp.float32)
        sts,vs=zip(*[open_slot(2*p,None),open_slot(2*p+1,on)])
        vs=[right_mul(*v,th,tl,0) for v in vs]
        vs=[left_mul(*v,th,tl,0) for v in vs]
        vs=[middle(st,v) for st,v in zip(sts,vs)]
        vs=[right_mul(*v,th,tl,1) for v in vs]
        vs=[left_mul(*v,th,tl,1) for v in vs]
        for st,v in zip(sts,vs): close_slot(st,v)
        return 0
    lax.fori_loop(0,(live[0,0]+1)//2,pair,0)

def compute(offs,live,ext,probe,meas,hi,lo):
    f=jnp.float32
    sd=jax.ShapeDtypeStruct
    V=pl.BlockSpec(memory_space=pltpu.VMEM); M=pl.BlockSpec(memory_space=pltpu.SMEM)
    return pl.pallas_call(kernel,
        out_shape=[sd((2,6,T+W,128),f),sd((3,W,W),f)],
        in_specs=[M,M,V,V,V,V,V],out_specs=[V,V],
        compiler_params=pltpu.CompilerParams(vmem_limit_bytes=VM2*2**20),
    )(jnp.swapaxes(offs,2,3),live,ext,probe,meas,hi,lo)


VM1, VM3, NC = 4, 16, 64


MESH = pl.DeviceIdType.MESH


def put(src, dst, send, recv, device):
    return pltpu.make_async_remote_copy(src_ref=src, dst_ref=dst, send_sem=send, recv_sem=recv, device_id=device, device_id_type=MESH)


def places():
    row, col = lax.axis_index("row"), lax.axis_index("col")
    rows, cols = lax.axis_size("row"), lax.axis_size("col")
    return row, col, ((row + rows - 1) % rows, col), ((row + 1) % rows, col), (row, (col + cols - 1) % cols), (row, (col + 1) % cols)


def greet(devices):
    barrier = pltpu.get_barrier_semaphore()
    for device in devices:
        pl.semaphore_signal(barrier, inc=1, device_id=device, device_id_type=MESH)
    return barrier


def halo_kernel(tile, probe, meas, th, tl, ext, probev, measv, thv, tlv, hop1, hop2, loc, snd, rcv):
    row, col, up, down, left, right = places()
    loads = []

    def load(src, dst):
        c = pltpu.make_async_copy(src, dst, loc.at[len(loads)])
        loads.append(c)
        c.start()

    barrier = greet((right, up, down))
    pl.semaphore_wait(barrier, 3)
    n = [0]
    sent = []

    def send(src, dst, device):
        k = n[0]
        n[0] += 1
        c = put(src, dst, snd.at[k], rcv.at[k], device)
        c.start()
        sent.append(c)
        return c

    def lanes(cb):
        return pl.ds(128 * cb, 128)

    H = W // 2
    low = pl.ds(T, W)
    far = [pl.ds(T + H * k, H) for k in range(2)]
    first = [send(tile.at[:, pl.ds(H * k, H), lanes(3)], hop1.at[k], down) for k in range(2)]
    b = [send(tile.at[:, pl.ds(0, W), lanes(cb)], ext.at[:, cb, low, :], up) for cb in range(2)]
    r = [send(tile.at[:, :, lanes(cb)], ext.at[:, 4 + cb, pl.ds(0, T), :], left) for cb in range(2)]
    b2 = send(tile.at[:, pl.ds(0, W), lanes(2)], ext.at[:, 2, low, :], up)
    for cb in range(4):
        load(tile.at[:, :, lanes(cb)], ext.at[:, cb, pl.ds(0, T), :])
    for src, dst in ((probe, probev), (meas, measv), (th, thv), (tl, tlv)):
        load(src, dst)
    second, third, x = [], [], []
    for k in range(2):
        first[k].wait_recv()
        second.append(send(hop1.at[k], hop2.at[k], down))
    for k in range(2):
        b[k].wait_recv()
        x.append(send(ext.at[:, k, low, :], ext.at[:, 4 + k, low, :], left))
        second[k].wait_recv()
        third.append(send(hop2.at[k], ext.at[:, 3, far[k], :], down))
    for c in loads:
        c.wait()
    for c in (*r, b2, *third, *x):
        c.wait_recv()
    for c in sent:
        c.wait_send()


def halos(tile, probe, meas, th, tl):
    f = jnp.float32
    A = pl.BlockSpec(memory_space=pl.ANY)
    sd = jax.ShapeDtypeStruct
    H = W // 2
    same = [sd(a.shape, a.dtype) for a in (probe, meas, th, tl)]
    return pl.pallas_call(lambda *a: halo_kernel(*a), out_shape=[sd((2, 6, T + W, 128), f), *same],
        in_specs=[pl.BlockSpec(memory_space=pltpu.HBM)] * 5, out_specs=[A] * 5,
        scratch_shapes=[pltpu.VMEM((2, 2, H, 128), f), pltpu.VMEM((2, 2, H, 128), f), pltpu.SemaphoreType.DMA((8,)), pltpu.SemaphoreType.DMA((13,)), pltpu.SemaphoreType.DMA((13,))],
        compiler_params=pltpu.CompilerParams(collective_id=0, has_side_effects=True, vmem_limit_bytes=VM1*2**20))(*[pltpu.with_memory_space_constraint(a, pltpu.HBM) for a in (tile, probe, meas, th, tl)])


GIVE = ((0, 1), (2,), (3,))


def spill_kernel(g, pg, rrv, brv, step, hop1, hop2, zhop1, zhop2, corner, bleft, mine, half, acc, plane, part, ybuf, shard, loc, snd, rcv, psnd, prcv, gsnd, grcv, fsnd, frcv, zsnd, zrcv):
    row, col, up, down, left, right = places()
    rows, depth = lax.axis_size("row"), 4
    chips = lax.axis_size("col") // 2
    wide = chips // depth
    core, chip = col % 2, col // 2
    x, z = chip // depth, chip % depth
    H = W // 2
    step_rows = H // chips

    def at(xx, zz, cc):
        return (row, ((xx % wide) * depth + zz % depth) * 2 + cc)

    def peer(j):
        return (row, ((chip + j) % chips) * 2 + core)

    sib = at(x, z, 1 - core)
    zm = at(x, z + depth - 1, core)
    around = at(x + jnp.where(z == 1, 1, 0), z + depth - 1, 0)
    source = at(x + jnp.where(z == 0, wide - 1, 0), z + 1, 1)
    ys = [((row + k) % rows, col) for k in range(1, 4)]
    barrier = greet((left, sib, *ys))

    @pl.when(core == 0)
    def _():
        pl.semaphore_signal(barrier, inc=1, device_id=source, device_id_type=MESH)

    def hello(j, _):
        pl.semaphore_signal(barrier, inc=1, device_id=peer(j), device_id_type=MESH)
        return 0

    lax.fori_loop(1, chips, hello, 0)
    loads = []

    def load(src, dst):
        c = pltpu.make_async_copy(src, dst, loc.at[len(loads)])
        loads.append(c)
        c.start()
        return c

    def block(start, size):
        return pl.ds(pl.multiple_of(start, size), size)

    low, top = pl.ds(T, W), pl.ds(0, T)
    l_mine = load(pg.at[:, block(core * H, H), :], mine)
    l_left = load(g.at[:, pl.ds(0, 2), low, :], bleft)
    pl.semaphore_wait(barrier, 5 + chips - 1 + core)
    n = [0]
    sent = []

    def send(src, dst, device):
        k = n[0]
        n[0] += 1
        c = put(src, dst, snd.at[k], rcv.at[k], device)
        c.start()
        sent.append(c)
        return c

    s1 = send(pg.at[:, block((1 - core) * H, H), :], half, sib)
    cuts = [pl.ds(NC * k, NC) for k in range(W // NC)]
    sc = [send(g.at[:, 4:6, pl.ds(T + NC * k, NC), :], corner.at[:, :, cuts[k], :], right) for k in range(W // NC)]
    far = [pl.ds(H * k, H) for k in range(2)]
    first = [send(g.at[:, 3, pl.ds(T + H * k, H), :], hop1.at[k], up) for k in range(2)]
    b2 = send(g.at[:, 2, low, :], brv.at[:, 2], down)
    zrows = [pl.ds(H * (k + 1), H) for k in range(3)]

    def zcopy(level, k):
        if level == 0:
            return put(g.at[:, 5, zrows[k], :], zhop1.at[k], zsnd.at[k], zrcv.at[k], zm)
        if level == 1:
            return put(zhop1.at[k], zhop2.at[k], zsnd.at[3 + k], zrcv.at[3 + k], zm)
        return put(zhop2.at[k], rrv.at[:, 1, zrows[k], :], zsnd.at[6 + k], zrcv.at[6 + k], around)

    def zdirect(k):
        return put(g.at[:, 5, zrows[k], :], rrv.at[:, 1, zrows[k], :], zsnd.at[k], zrcv.at[6 + k], sib)

    l_mine.wait()
    s1.wait_recv()
    acc[...] = mine[...] + half[...]

    def shard_of(j):
        p = (chip + j) % chips
        return put(acc.at[:, block(p * step_rows, step_rows), :], plane.at[j], psnd.at[j], prcv.at[j], peer(j))

    def begin(j, _):
        shard_of(j).start()
        return 0

    lax.fori_loop(1, chips, begin, 0)
    @pl.when(core == 1)
    def _():
        for k in range(3):
            zcopy(0, k).start()

    @pl.when(core == 0)
    def _():
        for k in range(3):
            zdirect(k).start()

    r = [send(g.at[:, 4, top, :], rrv.at[:, 0], right), send(g.at[:, 5, pl.ds(0, H), :], rrv.at[:, 1, pl.ds(0, H), :], right)]
    l_left.wait()
    b, second, third = [], [], []
    def give(k):
        sc[k].wait_recv()
        bleft[:, :, cuts[k], :] += corner[:, :, cuts[k], :]
        b.append(send(bleft.at[:, :, cuts[k], :], brv.at[:, 0:2, cuts[k], :], down))

    for k in GIVE[0]:
        give(k)
    for j in range(2):
        first[j].wait_recv()
        second.append(send(hop1.at[j], hop2.at[j], up))

    @pl.when(core == 1)
    def _():
        for k in range(3):
            zcopy(0, k).wait_recv()
            zcopy(1, k).start()

    part[...] = acc[:, block(chip * step_rows, step_rows), :]

    def collect(j, _):
        shard_of(j).wait_recv()
        part[...] += plane[j]
        return 0

    lax.fori_loop(1, chips, collect, 0)
    yr = [send(part, ybuf.at[row], ys[k]) for k in range(3)]
    ybuf[pl.ds(row, 1)] = part[...][None]
    for k in GIVE[1]:
        give(k)
    for c in yr:
        c.wait_recv()
    total = ybuf[0] + ybuf[1] + ybuf[2] + ybuf[3]
    shard[...] = total[:2] / jnp.sqrt(total[2:])
    here = block(core * H + chip * step_rows, step_rows)

    own = load(shard, step.at[:, here, :])

    def gather(j):
        return put(shard, step.at[:, here, :], gsnd.at[j], grcv.at[j], peer(j))

    def begin2(j, _):
        gather(j).start()
        return 0

    lax.fori_loop(1, chips, begin2, 0)

    def pass_on(j):
        rows_j = block(core * H + (chip + chips - j) % chips * step_rows, step_rows)
        return put(step.at[:, rows_j, :], step.at[:, rows_j, :], fsnd.at[j], frcv.at[j], sib)

    own.wait()
    pass_on(0).start()
    for k in GIVE[2]:
        give(k)
    for k in range(2):
        second[k].wait_recv()
        third.append(send(hop2.at[k], brv.at[:, 3, far[k], :], up))

    @pl.when(core == 1)
    def _():
        for k in range(3):
            zcopy(1, k).wait_recv()
            zcopy(2, k).start()


    def collect2(j, _):
        gather(j).wait_recv()
        pass_on(j).start()
        return 0

    lax.fori_loop(1, chips, collect2, 0)
    for c in (*r, b2, *b, *third):
        c.wait_recv()
    for k in range(3):
        zcopy(2, k).wait_recv()

    def collect3(j, _):
        pass_on(j).wait_recv()
        pass_on(j).wait_send()
        return 0

    lax.fori_loop(0, chips, collect3, 0)

    def drain(j, _):
        shard_of(j).wait_send()
        gather(j).wait_send()
        return 0

    lax.fori_loop(1, chips, drain, 0)
    for c in sent:
        c.wait_send()

    @pl.when(core == 1)
    def _():
        for level in range(3):
            for k in range(3):
                zcopy(level, k).wait_send()

    @pl.when(core == 0)
    def _():
        for k in range(3):
            zdirect(k).wait_send()


def spills(g, pg, rows, cols):
    f = jnp.float32
    A = pl.BlockSpec(memory_space=pl.ANY)
    sd = jax.ShapeDtypeStruct
    V = pltpu.VMEM
    D = pltpu.SemaphoreType.DMA
    H = W // 2
    chips = cols // 2
    sh = H // chips
    return pl.pallas_call(lambda *a: spill_kernel(*a), out_shape=[sd((2, 2, T, 128), f), sd((2, 4, W, 128), f), sd((2, W, W), f)],
        in_specs=[A] * 2, out_specs=[A] * 3,
        scratch_shapes=[V((2, 2, H, 128), f), V((2, 2, H, 128), f), V((3, 2, H, 128), f), V((3, 2, H, 128), f), V((2, 2, W, 128), f), V((2, 2, W, 128), f),
            V((3, H, W), f), V((3, H, W), f), V((3, H, W), f), V((chips, 3, sh, W), f), V((3, sh, W), f), V((rows, 3, sh, W), f), V((2, sh, W), f),
            D((4,)), D((40,)), D((40,)), *[D((chips,))] * 6, D((9,)), D((9,))],
        compiler_params=pltpu.CompilerParams(collective_id=1, has_side_effects=True, vmem_limit_bytes=VM3*2**20))(g, pg)


def join_kernel(g, rrv, brv, stepv, grad, step, out, sem):
    s = pltpu.make_async_copy(stepv, step, sem.at[4])
    s.start()
    cps = []
    for cb in (3, 2, 1, 0):
        for k in range(4):
            at_rows = pl.ds(128 * k, 128)
            v = g[:, cb, at_rows, :]
            if cb < 2:
                v = v + rrv[:, cb, at_rows, :]
            if k < 2:
                v = v + brv[:, cb, at_rows, :]
            out[:, cb, at_rows, :] = v
        cps.append(pltpu.make_async_copy(out.at[:, cb], grad.at[:, :, pl.ds(128 * cb, 128)], sem.at[cb]))
        cps[-1].start()
    for c in (s, *cps):
        c.wait()


def join(g, rrv, brv, stepv):
    f = jnp.float32
    V = pl.BlockSpec(memory_space=pltpu.VMEM)
    A = pl.BlockSpec(memory_space=pl.ANY)
    sd = jax.ShapeDtypeStruct
    return pl.pallas_call(join_kernel, out_shape=[sd((2, T, T), f), sd((2, W, W), f)],
        in_specs=[V, V, V, V], out_specs=[A, A],
        scratch_shapes=[pltpu.VMEM((2, 4, T, 128), f), pltpu.SemaphoreType.DMA((5,))],
        compiler_params=pltpu.CompilerParams(vmem_limit_bytes=16*2**20))(g, rrv, brv, stepv)


def local(specimen, probe_field, measured, offsets, live_counts):
    hi, lo = tables()
    ext, probe, meas, hi, lo = halos(specimen, probe_field, measured[0, 0], jnp.asarray(hi), jnp.asarray(lo))
    g, pg = compute(offsets, live_counts, ext, probe, meas, hi, lo)
    rrv, brv, step = spills(g, pg, lax.axis_size("row"), lax.axis_size("col"))
    return tuple(join(g, rrv, brv, step))


def solution(mesh):
    from jax.sharding import PartitionSpec as P
    in_specs = (P(None, "row", "col"), P(), P("row", "col", None, None, None), P("row", "col", None, None), P("row", "col"))
    out_specs = (P(None, "row", "col"), P())
    return jax.shard_map(local, mesh=mesh, in_specs=in_specs, out_specs=out_specs, check_vma=False)
```

```python
import functools, math
import jax, jax.numpy as jnp, numpy as np, ml_dtypes
from jax import lax
from jax.experimental import pallas as pl
from jax.experimental.pallas import tpu as pltpu

W=256; T=512; S=8
VM2=24
R=32
BF=jnp.bfloat16
def tables():
    k=np.arange(W); k=np.where(k<W//2,k,k-W).astype(np.float64)
    h=np.exp(-1j*math.pi*0.25*k*k/W)
    a=np.fft.ifft(h)
    H=W//2
    d=(np.arange(H)[:,None]-np.arange(H)[None,:])
    out=[]
    for sgn in (1,-1):
        c=0.5*(a[d%W]+sgn*a[(d+H)%W])
        ml=np.block([[c.real,-c.imag],[c.imag,c.real]])
        out.append(ml)
    ml=np.stack(out)
    mr=np.swapaxes(ml,1,2)
    def split(m):
        hi=m.astype(np.float32).astype(ml_dtypes.bfloat16)
        lo=(m-hi.astype(np.float64)).astype(np.float32).astype(ml_dtypes.bfloat16)
        return hi,lo
    lh,ll=split(ml); rh,rl=split(mr)
    return np.stack([lh,rh]),np.stack([ll,rl])

def split(x):
    hi=x.astype(BF)
    lo=(x-hi.astype(jnp.float32)).astype(BF)
    return hi,lo

def right_mul(xr,xi,th,tl,which):
    H=W//2
    outs=[]
    for n,(r,i) in enumerate(((xr[:,:H]+xr[:,H:],xi[:,:H]+xi[:,H:]),(xr[:,:H]-xr[:,H:],xi[:,:H]-xi[:,H:]))):
        s=jnp.concatenate([r,i],axis=1)
        hi,lo=split(s)
        lhs=jnp.concatenate([hi,hi,lo],axis=1)
        outs.append(jnp.dot(lhs,jnp.concatenate([th[1-which,n],tl[1-which,n],th[1-which,n]],axis=0),preferred_element_type=jnp.float32))
    u,v=outs
    yr=jnp.concatenate([u[:,:H]+v[:,:H],u[:,:H]-v[:,:H]],axis=1)
    yi=jnp.concatenate([u[:,H:]+v[:,H:],u[:,H:]-v[:,H:]],axis=1)
    return yr,yi

def left_mul(xr,xi,th,tl,which):
    H=W//2
    outs=[]
    for n,(r,i) in enumerate(((xr[:H]+xr[H:],xi[:H]+xi[H:]),(xr[:H]-xr[H:],xi[:H]-xi[H:]))):
        s=jnp.concatenate([r,i],axis=0)
        hi,lo=split(s)
        rhs=jnp.concatenate([hi,lo,hi],axis=0)
        outs.append(jnp.dot(jnp.concatenate([th[which,n],th[which,n],tl[which,n]],axis=1),rhs,preferred_element_type=jnp.float32))
    u,v=outs
    yr=jnp.concatenate([u[:H]+v[:H],u[:H]-v[:H]],axis=0)
    yi=jnp.concatenate([u[H:]+v[H:],u[H:]-v[H:]],axis=0)
    return yr,yi

def kernel(offs,live,ext,probe,mv,th,tl,g0,pg0, grad,pg,win):
    H=W//2
    def dd(a,b): return jnp.dot(a,b,preferred_element_type=jnp.float32)
    def cols(r,i):
        return [split(jnp.concatenate([f(r[:,:H],r[:,H:]),f(i[:,:H],i[:,H:])],axis=1)) for f in (jnp.add,jnp.subtract)]
    def stack(parts): return jnp.concatenate(parts,axis=0)
    def right(parts,which):
        out=[]
        for n in range(2):
            hi=stack([p[n][0] for p in parts]); lo=stack([p[n][1] for p in parts])
            p=dd(jnp.concatenate([hi,lo],axis=0),th[1-which,n])
            out.append(p[:W]+p[W:]+dd(hi,tl[1-which,n]))
        return out
    def left(uv,which):
        u,v=uv
        re=[[],[]]; im=[[],[]]
        for c in range(0,H,R):
            def y(r):
                a=u[r:r+R]; b=v[r:r+R]
                p=a+b; m=a-b
                return jnp.concatenate([p[:,:H],m[:,:H]],axis=1),jnp.concatenate([p[:,H:],m[:,H:]],axis=1)
            (tr,ti),(br,bi)=y(c),y(c+H)
            for n,f in enumerate((jnp.add,jnp.subtract)):
                re[n].append(split(f(tr,br))); im[n].append(split(f(ti,bi)))
        out=[]
        for n in range(2):
            hi=stack([p[0] for p in re[n]]+[p[0] for p in im[n]]); lo=stack([p[1] for p in re[n]]+[p[1] for p in im[n]])
            p=dd(jnp.concatenate([th[which,n],tl[which,n]],axis=0),hi)
            out.append(p[:W]+p[W:]+dd(th[which,n],lo))
        return out
    def rows(uv):
        u,v=uv
        for c in range(0,H,R):
            ur,ui,vr,vi=u[c:c+R],u[H+c:H+c+R],v[c:c+R],v[H+c:H+c+R]
            yield c,ur+vr,ui+vi
            yield c+H,ur-vr,ui-vi
    def place(s):
        r0=offs[0,0,0,s]; c0=offs[0,0,1,s]
        q=c0//128
        return r0,q,c0-q*128
    lane=lax.broadcasted_iota(jnp.int32,(R,128),1)
    def begin(n,s):
        r0,q,sh=place(s)
        keep=lane<128-sh
        parts=[]
        for c in range(0,W,R):
            o=[]
            for ch in range(2):
                x=[pltpu.roll(ext[ch,q+j,pl.ds(r0+c,R),:],128-sh,1) for j in range(3)]
                o.append(jnp.concatenate([jnp.where(keep,x[0],x[1]),jnp.where(keep,x[1],x[2])],axis=1))
                win[n,ch,c:c+R,:]=o[ch]
            a,b=o; pr=probe[0,c:c+R,:]; pi=probe[1,c:c+R,:]
            parts.append(cols(pr*a-pi*b,pr*b+pi*a))
        return parts
    def middle(uv,s,on):
        parts={}
        for c,yr,yi in rows(uv):
            res=yr*yr+yi*yi-mv[s,c:c+R,:]
            if on is not None: res=res*on
            parts[c]=cols(res*yr,res*yi)
        return [parts[c] for c in sorted(parts)]
    def finish(n,uv,s,on):
        r0,q,sh=place(s)
        low=lane<sh
        for c,br,bi in rows(uv):
            a=win[n,0,c:c+R,:]; b=win[n,1,c:c+R,:]
            pr=probe[0,c:c+R,:]; pi=probe[1,c:c+R,:]
            pg[0,c:c+R,:]+=a*br+b*bi
            pg[1,c:c+R,:]+=a*bi-b*br
            il=a*a+b*b
            pg[2,c:c+R,:]+=il if on is None else il*on
            for ch,g in enumerate((pr*br+pi*bi,pr*bi-pi*br)):
                x=pltpu.roll(g[:,:128],sh,1); y=pltpu.roll(g[:,128:],sh,1)
                z=jnp.zeros_like(x)
                at=pl.ds(r0+c,R)
                grad[ch,q,at,:]+=jnp.where(low,z,x)
                grad[ch,q+1,at,:]+=jnp.where(low,x,y)
                grad[ch,q+2,at,:]+=jnp.where(low,y,z)
    def pair(p,_):
        two=[(0,2*p,None),(1,2*p+1,(2*p+1<live[0,0]).astype(jnp.float32))]
        v=[right(begin(n,s),0) for n,s,_ in two]
        v=[left(x,0) for x in v]
        v=[right(middle(x,s,on),1) for x,(n,s,on) in zip(v,two)]
        v=[left(x,1) for x in v]
        for x,(n,s,on) in zip(v,two): finish(n,x,s,on)
        return 0
    lax.fori_loop(0,(live[0,0]+1)//2,pair,0)

def compute(offs,live,ext,probe,meas,hi,lo,g0,pg0):
    f=jnp.float32
    sd=jax.ShapeDtypeStruct
    V=pl.BlockSpec(memory_space=pltpu.VMEM); M=pl.BlockSpec(memory_space=pltpu.SMEM)
    return pl.pallas_call(kernel,
        out_shape=[sd((2,6,T+W,128),f),sd((3,W,W),f)],
        in_specs=[M,M,V,V,V,V,V,V,V],out_specs=[V,V],input_output_aliases={7:0,8:1},scratch_shapes=[pltpu.VMEM((2,2,W,W),f)],
        compiler_params=pltpu.CompilerParams(vmem_limit_bytes=VM2*2**20),
    )(jnp.swapaxes(offs,2,3),live,ext,probe,meas,hi,lo,g0,pg0)


VM1, VM3, NC = 4, 16, 64


MESH = pl.DeviceIdType.MESH


def put(src, dst, send, recv, device):
    return pltpu.make_async_remote_copy(src_ref=src, dst_ref=dst, send_sem=send, recv_sem=recv, device_id=device, device_id_type=MESH)


def places():
    row, col = lax.axis_index("row"), lax.axis_index("col")
    rows, cols = lax.axis_size("row"), lax.axis_size("col")
    return row, col, ((row + rows - 1) % rows, col), ((row + 1) % rows, col), (row, (col + cols - 1) % cols), (row, (col + 1) % cols)


def greet(devices):
    barrier = pltpu.get_barrier_semaphore()
    for device in devices:
        pl.semaphore_signal(barrier, inc=1, device_id=device, device_id_type=MESH)
    return barrier


def halo_kernel(tile, probe, meas, th, tl, ext, probev, measv, thv, tlv, g0, pg0, hop1, hop2, zg, zp, loc, snd, rcv):
    row, col, up, down, left, right = places()
    loads = []

    def load(src, dst):
        c = pltpu.make_async_copy(src, dst, loc.at[len(loads)])
        loads.append(c)
        c.start()

    barrier = greet((right, up, down))
    pl.semaphore_wait(barrier, 3)
    n = [0]
    sent = []

    def send(src, dst, device):
        k = n[0]
        n[0] += 1
        c = put(src, dst, snd.at[k], rcv.at[k], device)
        c.start()
        sent.append(c)
        return c

    def lanes(cb):
        return pl.ds(128 * cb, 128)

    H = W // 2
    low = pl.ds(T, W)
    far = [pl.ds(T + H * k, H) for k in range(2)]
    first = [send(tile.at[:, pl.ds(H * k, H), lanes(3)], hop1.at[k], down) for k in range(2)]
    b = [send(tile.at[:, pl.ds(0, W), lanes(cb)], ext.at[:, cb, low, :], up) for cb in range(2)]
    r = [send(tile.at[:, :, lanes(cb)], ext.at[:, 4 + cb, pl.ds(0, T), :], left) for cb in range(2)]
    b2 = send(tile.at[:, pl.ds(0, W), lanes(2)], ext.at[:, 2, low, :], up)
    for cb in range(4):
        load(tile.at[:, :, lanes(cb)], ext.at[:, cb, pl.ds(0, T), :])
    for src, dst in ((probe, probev), (meas, measv), (th, thv), (tl, tlv)):
        load(src, dst)
    zg[...] = jnp.zeros_like(zg)
    zp[...] = jnp.zeros_like(zp)
    for cb in range(6):
        load(zg, g0.at[:, cb])
    load(zp, pg0)
    second, third, x = [], [], []
    for k in range(2):
        first[k].wait_recv()
        second.append(send(hop1.at[k], hop2.at[k], down))
    for k in range(2):
        b[k].wait_recv()
        x.append(send(ext.at[:, k, low, :], ext.at[:, 4 + k, low, :], left))
        second[k].wait_recv()
        third.append(send(hop2.at[k], ext.at[:, 3, far[k], :], down))
    for c in loads:
        c.wait()
    for c in (*r, b2, *third, *x):
        c.wait_recv()
    for c in sent:
        c.wait_send()


def halos(tile, probe, meas, th, tl):
    f = jnp.float32
    A = pl.BlockSpec(memory_space=pl.ANY)
    sd = jax.ShapeDtypeStruct
    H = W // 2
    same = [sd(a.shape, a.dtype) for a in (probe, meas, th, tl)]
    return pl.pallas_call(lambda *a: halo_kernel(*a), out_shape=[sd((2, 6, T + W, 128), f), *same, sd((2, 6, T + W, 128), f), sd((3, W, W), f)],
        in_specs=[pl.BlockSpec(memory_space=pltpu.HBM)] * 5, out_specs=[A] * 7,
        scratch_shapes=[pltpu.VMEM((2, 2, H, 128), f), pltpu.VMEM((2, 2, H, 128), f), pltpu.VMEM((2, T + W, 128), f), pltpu.VMEM((3, W, W), f), pltpu.SemaphoreType.DMA((16,)), pltpu.SemaphoreType.DMA((13,)), pltpu.SemaphoreType.DMA((13,))],
        compiler_params=pltpu.CompilerParams(collective_id=0, has_side_effects=True, vmem_limit_bytes=VM1*2**20))(*[pltpu.with_memory_space_constraint(a, pltpu.HBM) for a in (tile, probe, meas, th, tl)])


GIVE = ((0, 1), (2,), (3,))


def spill_kernel(g, pg, rrv, brv, step, hop1, hop2, zhop1, zhop2, corner, bleft, mine, half, acc, plane, part, ybuf, shard, loc, snd, rcv, psnd, prcv, gsnd, grcv, fsnd, frcv, zsnd, zrcv):
    row, col, up, down, left, right = places()
    rows, depth = lax.axis_size("row"), 4
    chips = lax.axis_size("col") // 2
    wide = chips // depth
    core, chip = col % 2, col // 2
    x, z = chip // depth, chip % depth
    H = W // 2
    step_rows = H // chips

    def at(xx, zz, cc):
        return (row, ((xx % wide) * depth + zz % depth) * 2 + cc)

    def peer(j):
        return (row, ((chip + j) % chips) * 2 + core)

    sib = at(x, z, 1 - core)
    zm = at(x, z + depth - 1, core)
    around = at(x + jnp.where(z == 1, 1, 0), z + depth - 1, 0)
    source = at(x + jnp.where(z == 0, wide - 1, 0), z + 1, 1)
    ys = [((row + k) % rows, col) for k in range(1, 4)]
    barrier = greet((left, sib, *ys))

    @pl.when(core == 0)
    def _():
        pl.semaphore_signal(barrier, inc=1, device_id=source, device_id_type=MESH)

    def hello(j, _):
        pl.semaphore_signal(barrier, inc=1, device_id=peer(j), device_id_type=MESH)
        return 0

    lax.fori_loop(1, chips, hello, 0)
    loads = []

    def load(src, dst):
        c = pltpu.make_async_copy(src, dst, loc.at[len(loads)])
        loads.append(c)
        c.start()
        return c

    def block(start, size):
        return pl.ds(pl.multiple_of(start, size), size)

    low, top = pl.ds(T, W), pl.ds(0, T)
    l_mine = load(pg.at[:, block(core * H, H), :], mine)
    l_left = load(g.at[:, pl.ds(0, 2), low, :], bleft)
    pl.semaphore_wait(barrier, 5 + chips - 1 + core)
    n = [0]
    sent = []

    def send(src, dst, device):
        k = n[0]
        n[0] += 1
        c = put(src, dst, snd.at[k], rcv.at[k], device)
        c.start()
        sent.append(c)
        return c

    s1 = send(pg.at[:, block((1 - core) * H, H), :], half, sib)
    cuts = [pl.ds(NC * k, NC) for k in range(W // NC)]
    sc = [send(g.at[:, 4:6, pl.ds(T + NC * k, NC), :], corner.at[:, :, cuts[k], :], right) for k in range(W // NC)]
    far = [pl.ds(H * k, H) for k in range(2)]
    first = [send(g.at[:, 3, pl.ds(T + H * k, H), :], hop1.at[k], up) for k in range(2)]
    b2 = send(g.at[:, 2, low, :], brv.at[:, 2], down)
    zrows = [pl.ds(H * (k + 1), H) for k in range(3)]

    def zcopy(level, k):
        if level == 0:
            return put(g.at[:, 5, zrows[k], :], zhop1.at[k], zsnd.at[k], zrcv.at[k], zm)
        if level == 1:
            return put(zhop1.at[k], zhop2.at[k], zsnd.at[3 + k], zrcv.at[3 + k], zm)
        return put(zhop2.at[k], rrv.at[:, 1, zrows[k], :], zsnd.at[6 + k], zrcv.at[6 + k], around)

    def zdirect(k):
        return put(g.at[:, 5, zrows[k], :], rrv.at[:, 1, zrows[k], :], zsnd.at[k], zrcv.at[6 + k], sib)

    l_mine.wait()
    s1.wait_recv()
    acc[...] = mine[...] + half[...]

    def shard_of(j):
        p = (chip + j) % chips
        return put(acc.at[:, block(p * step_rows, step_rows), :], plane.at[j], psnd.at[j], prcv.at[j], peer(j))

    def begin(j, _):
        shard_of(j).start()
        return 0

    lax.fori_loop(1, chips, begin, 0)
    @pl.when(core == 1)
    def _():
        for k in range(3):
            zcopy(0, k).start()

    @pl.when(core == 0)
    def _():
        for k in range(3):
            zdirect(k).start()

    r = [send(g.at[:, 4, top, :], rrv.at[:, 0], right), send(g.at[:, 5, pl.ds(0, H), :], rrv.at[:, 1, pl.ds(0, H), :], right)]
    l_left.wait()
    b, second, third = [], [], []
    def give(k):
        sc[k].wait_recv()
        bleft[:, :, cuts[k], :] += corner[:, :, cuts[k], :]
        b.append(send(bleft.at[:, :, cuts[k], :], brv.at[:, 0:2, cuts[k], :], down))

    for k in GIVE[0]:
        give(k)
    for j in range(2):
        first[j].wait_recv()
        second.append(send(hop1.at[j], hop2.at[j], up))

    @pl.when(core == 1)
    def _():
        for k in range(3):
            zcopy(0, k).wait_recv()
            zcopy(1, k).start()

    part[...] = acc[:, block(chip * step_rows, step_rows), :]

    def collect(j, _):
        shard_of(j).wait_recv()
        part[...] += plane[j]
        return 0

    lax.fori_loop(1, chips, collect, 0)
    yr = [send(part, ybuf.at[row], ys[k]) for k in range(3)]
    ybuf[pl.ds(row, 1)] = part[...][None]
    for k in GIVE[1]:
        give(k)
    for c in yr:
        c.wait_recv()
    total = ybuf[0] + ybuf[1] + ybuf[2] + ybuf[3]
    shard[...] = total[:2] / jnp.sqrt(total[2:])
    here = block(core * H + chip * step_rows, step_rows)

    own = load(shard, step.at[:, here, :])

    def gather(j):
        return put(shard, step.at[:, here, :], gsnd.at[j], grcv.at[j], peer(j))

    def begin2(j, _):
        gather(j).start()
        return 0

    lax.fori_loop(1, chips, begin2, 0)

    def pass_on(j):
        rows_j = block(core * H + (chip + chips - j) % chips * step_rows, step_rows)
        return put(step.at[:, rows_j, :], step.at[:, rows_j, :], fsnd.at[j], frcv.at[j], sib)

    own.wait()
    pass_on(0).start()
    for k in GIVE[2]:
        give(k)
    for k in range(2):
        second[k].wait_recv()
        third.append(send(hop2.at[k], brv.at[:, 3, far[k], :], up))

    @pl.when(core == 1)
    def _():
        for k in range(3):
            zcopy(1, k).wait_recv()
            zcopy(2, k).start()


    def collect2(j, _):
        gather(j).wait_recv()
        pass_on(j).start()
        return 0

    lax.fori_loop(1, chips, collect2, 0)
    for c in (*r, b2, *b, *third):
        c.wait_recv()
    for k in range(3):
        zcopy(2, k).wait_recv()

    def collect3(j, _):
        pass_on(j).wait_recv()
        pass_on(j).wait_send()
        return 0

    lax.fori_loop(0, chips, collect3, 0)

    def drain(j, _):
        shard_of(j).wait_send()
        gather(j).wait_send()
        return 0

    lax.fori_loop(1, chips, drain, 0)
    for c in sent:
        c.wait_send()

    @pl.when(core == 1)
    def _():
        for level in range(3):
            for k in range(3):
                zcopy(level, k).wait_send()

    @pl.when(core == 0)
    def _():
        for k in range(3):
            zdirect(k).wait_send()


def spills(g, pg, rows, cols):
    f = jnp.float32
    A = pl.BlockSpec(memory_space=pl.ANY)
    sd = jax.ShapeDtypeStruct
    V = pltpu.VMEM
    D = pltpu.SemaphoreType.DMA
    H = W // 2
    chips = cols // 2
    sh = H // chips
    return pl.pallas_call(lambda *a: spill_kernel(*a), out_shape=[sd((2, 2, T, 128), f), sd((2, 4, W, 128), f), sd((2, W, W), f)],
        in_specs=[A] * 2, out_specs=[A] * 3,
        scratch_shapes=[V((2, 2, H, 128), f), V((2, 2, H, 128), f), V((3, 2, H, 128), f), V((3, 2, H, 128), f), V((2, 2, W, 128), f), V((2, 2, W, 128), f),
            V((3, H, W), f), V((3, H, W), f), V((3, H, W), f), V((chips, 3, sh, W), f), V((3, sh, W), f), V((rows, 3, sh, W), f), V((2, sh, W), f),
            D((4,)), D((40,)), D((40,)), *[D((chips,))] * 6, D((9,)), D((9,))],
        compiler_params=pltpu.CompilerParams(collective_id=1, has_side_effects=True, vmem_limit_bytes=VM3*2**20))(g, pg)


def join_kernel(g, rrv, brv, stepv, grad, step, out, sem):
    s = pltpu.make_async_copy(stepv, step, sem.at[4])
    s.start()
    cps = []
    for cb in (3, 2, 1, 0):
        for k in range(4):
            at_rows = pl.ds(128 * k, 128)
            v = g[:, cb, at_rows, :]
            if cb < 2:
                v = v + rrv[:, cb, at_rows, :]
            if k < 2:
                v = v + brv[:, cb, at_rows, :]
            out[:, cb, at_rows, :] = v
        cps.append(pltpu.make_async_copy(out.at[:, cb], grad.at[:, :, pl.ds(128 * cb, 128)], sem.at[cb]))
        cps[-1].start()
    for c in (s, *cps):
        c.wait()


def join(g, rrv, brv, stepv):
    f = jnp.float32
    V = pl.BlockSpec(memory_space=pltpu.VMEM)
    A = pl.BlockSpec(memory_space=pl.ANY)
    sd = jax.ShapeDtypeStruct
    return pl.pallas_call(join_kernel, out_shape=[sd((2, T, T), f), sd((2, W, W), f)],
        in_specs=[V, V, V, V], out_specs=[A, A],
        scratch_shapes=[pltpu.VMEM((2, 4, T, 128), f), pltpu.SemaphoreType.DMA((5,))],
        compiler_params=pltpu.CompilerParams(vmem_limit_bytes=16*2**20))(g, rrv, brv, stepv)


def local(specimen, probe_field, measured, offsets, live_counts):
    hi, lo = tables()
    ext, probe, meas, hi, lo, g0, pg0 = halos(specimen, probe_field, measured[0, 0], jnp.asarray(hi), jnp.asarray(lo))
    g, pg = compute(offsets, live_counts, ext, probe, meas, hi, lo, g0, pg0)
    rrv, brv, step = spills(g, pg, lax.axis_size("row"), lax.axis_size("col"))
    return tuple(join(g, rrv, brv, step))


def solution(mesh):
    from jax.sharding import PartitionSpec as P
    in_specs = (P(None, "row", "col"), P(), P("row", "col", None, None, None), P("row", "col", None, None), P("row", "col"))
    out_specs = (P(None, "row", "col"), P())
    return jax.shard_map(local, mesh=mesh, in_specs=in_specs, out_specs=out_specs, check_vma=False)
```

```python
import functools, math
import jax, jax.numpy as jnp, numpy as np, ml_dtypes
from jax import lax
from jax.experimental import pallas as pl
from jax.experimental.pallas import tpu as pltpu

W=256; T=512; S=8
VM2=24
R=32
BF=jnp.bfloat16
def tables():
    k=np.arange(W); k=np.where(k<W//2,k,k-W).astype(np.float64)
    h=np.exp(-1j*math.pi*0.25*k*k/W)
    a=np.fft.ifft(h)
    H=W//2
    d=(np.arange(H)[:,None]-np.arange(H)[None,:])
    out=[]
    for sgn in (1,-1):
        c=0.5*(a[d%W]+sgn*a[(d+H)%W])
        ml=np.block([[c.real,-c.imag],[c.imag,c.real]])
        out.append(ml)
    ml=np.stack(out)
    mr=np.swapaxes(ml,1,2)
    def split(m):
        hi=m.astype(np.float32).astype(ml_dtypes.bfloat16)
        lo=(m-hi.astype(np.float64)).astype(np.float32).astype(ml_dtypes.bfloat16)
        return hi,lo
    lh,ll=split(ml); rh,rl=split(mr)
    return np.stack([lh,rh]),np.stack([ll,rl])

def split(x):
    hi=x.astype(BF)
    lo=(x-hi.astype(jnp.float32)).astype(BF)
    return hi,lo

def right_mul(xr,xi,th,tl,which):
    H=W//2
    outs=[]
    for n,(r,i) in enumerate(((xr[:,:H]+xr[:,H:],xi[:,:H]+xi[:,H:]),(xr[:,:H]-xr[:,H:],xi[:,:H]-xi[:,H:]))):
        s=jnp.concatenate([r,i],axis=1)
        hi,lo=split(s)
        lhs=jnp.concatenate([hi,hi,lo],axis=1)
        outs.append(jnp.dot(lhs,jnp.concatenate([th[1-which,n],tl[1-which,n],th[1-which,n]],axis=0),preferred_element_type=jnp.float32))
    u,v=outs
    yr=jnp.concatenate([u[:,:H]+v[:,:H],u[:,:H]-v[:,:H]],axis=1)
    yi=jnp.concatenate([u[:,H:]+v[:,H:],u[:,H:]-v[:,H:]],axis=1)
    return yr,yi

def left_mul(xr,xi,th,tl,which):
    H=W//2
    outs=[]
    for n,(r,i) in enumerate(((xr[:H]+xr[H:],xi[:H]+xi[H:]),(xr[:H]-xr[H:],xi[:H]-xi[H:]))):
        s=jnp.concatenate([r,i],axis=0)
        hi,lo=split(s)
        rhs=jnp.concatenate([hi,lo,hi],axis=0)
        outs.append(jnp.dot(jnp.concatenate([th[which,n],th[which,n],tl[which,n]],axis=1),rhs,preferred_element_type=jnp.float32))
    u,v=outs
    yr=jnp.concatenate([u[:H]+v[:H],u[:H]-v[:H]],axis=0)
    yi=jnp.concatenate([u[H:]+v[H:],u[H:]-v[H:]],axis=0)
    return yr,yi

def kernel(offs,live,ext,probe,mv,th,tl,g0,pg0, grad,pg,win):
    H=W//2
    def dd(a,b): return jnp.dot(a,b,preferred_element_type=jnp.float32)
    def cols(r,i):
        return [split(jnp.concatenate([f(r[:,:H],r[:,H:]),f(i[:,:H],i[:,H:])],axis=1)) for f in (jnp.add,jnp.subtract)]
    def stack(parts): return jnp.concatenate(parts,axis=0)
    def right(parts,which):
        out=[]
        for n in range(2):
            hi=stack([p[n][0] for p in parts]); lo=stack([p[n][1] for p in parts])
            p=dd(jnp.concatenate([hi,lo],axis=0),th[1-which,n])
            out.append(p[:W]+p[W:]+dd(hi,tl[1-which,n]))
        return out
    def left(uv,which):
        u,v=uv
        re=[[],[]]; im=[[],[]]
        for c in range(0,H,R):
            def y(r):
                a=u[r:r+R]; b=v[r:r+R]
                p=a+b; m=a-b
                return jnp.concatenate([p[:,:H],m[:,:H]],axis=1),jnp.concatenate([p[:,H:],m[:,H:]],axis=1)
            (tr,ti),(br,bi)=y(c),y(c+H)
            for n,f in enumerate((jnp.add,jnp.subtract)):
                re[n].append(split(f(tr,br))); im[n].append(split(f(ti,bi)))
        out=[]
        for n in range(2):
            hi=stack([p[0] for p in re[n]]+[p[0] for p in im[n]]); lo=stack([p[1] for p in re[n]]+[p[1] for p in im[n]])
            p=dd(jnp.concatenate([th[which,n],tl[which,n]],axis=0),hi)
            out.append(p[:W]+p[W:]+dd(th[which,n],lo))
        return out
    def rows(uv):
        u,v=uv
        for c in range(0,H,R):
            ur,ui,vr,vi=u[c:c+R],u[H+c:H+c+R],v[c:c+R],v[H+c:H+c+R]
            yield c,ur+vr,ui+vi
            yield c+H,ur-vr,ui-vi
    def place(s):
        r0=offs[0,0,0,s]; c0=offs[0,0,1,s]
        q=c0//128
        return r0,q,c0-q*128
    lane=lax.broadcasted_iota(jnp.int32,(R,128),1)
    def begin(n,s):
        r0,q,sh=place(s)
        keep=lane<128-sh
        parts=[]
        for c in range(0,W,R):
            o=[]
            for ch in range(2):
                x=[pltpu.roll(ext[ch,q+j,pl.ds(r0+c,R),:],128-sh,1) for j in range(3)]
                o.append(jnp.concatenate([jnp.where(keep,x[0],x[1]),jnp.where(keep,x[1],x[2])],axis=1))
                win[n,ch,c:c+R,:]=o[ch]
            a,b=o; pr=probe[0,c:c+R,:]; pi=probe[1,c:c+R,:]
            parts.append(cols(pr*a-pi*b,pr*b+pi*a))
        return parts
    def middle(uv,s,on):
        parts={}
        for c,yr,yi in rows(uv):
            res=yr*yr+yi*yi-mv[s,c:c+R,:]
            if on is not None: res=res*on
            parts[c]=cols(res*yr,res*yi)
        return [parts[c] for c in sorted(parts)]
    def finish(n,uv,s,on):
        r0,q,sh=place(s)
        low=lane<sh
        for c,br,bi in rows(uv):
            a=win[n,0,c:c+R,:]; b=win[n,1,c:c+R,:]
            pr=probe[0,c:c+R,:]; pi=probe[1,c:c+R,:]
            pg[0,c:c+R,:]+=a*br+b*bi
            pg[1,c:c+R,:]+=a*bi-b*br
            il=a*a+b*b
            pg[2,c:c+R,:]+=il if on is None else il*on
            for ch,g in enumerate((pr*br+pi*bi,pr*bi-pi*br)):
                x=pltpu.roll(g[:,:128],sh,1); y=pltpu.roll(g[:,128:],sh,1)
                z=jnp.zeros_like(x)
                at=pl.ds(r0+c,R)
                grad[ch,q,at,:]+=jnp.where(low,z,x)
                grad[ch,q+1,at,:]+=jnp.where(low,x,y)
                grad[ch,q+2,at,:]+=jnp.where(low,y,z)
    def pair(p,_):
        two=[(0,2*p,None),(1,2*p+1,(2*p+1<live[0,0]).astype(jnp.float32))]
        v=[right(begin(n,s),0) for n,s,_ in two]
        v=[left(x,0) for x in v]
        v=[right(middle(x,s,on),1) for x,(n,s,on) in zip(v,two)]
        v=[left(x,1) for x in v]
        for x,(n,s,on) in zip(v,two): finish(n,x,s,on)
        return 0
    lax.fori_loop(0,(live[0,0]+1)//2,pair,0)

def compute(offs,live,ext,probe,meas,hi,lo,g0,pg0):
    f=jnp.float32
    sd=jax.ShapeDtypeStruct
    V=pl.BlockSpec(memory_space=pltpu.VMEM); M=pl.BlockSpec(memory_space=pltpu.SMEM)
    return pl.pallas_call(kernel,
        out_shape=[sd((2,6,T+W,128),f),sd((3,W,W),f)],
        in_specs=[M,M,V,V,V,V,V,V,V],out_specs=[V,V],input_output_aliases={7:0,8:1},scratch_shapes=[pltpu.VMEM((2,2,W,W),f)],
        compiler_params=pltpu.CompilerParams(vmem_limit_bytes=VM2*2**20),
    )(jnp.swapaxes(offs,2,3),live,ext,probe,meas,hi,lo,g0,pg0)


VM1, VM3, NC = 4, 16, 64


MESH = pl.DeviceIdType.MESH


def put(src, dst, send, recv, device):
    return pltpu.make_async_remote_copy(src_ref=src, dst_ref=dst, send_sem=send, recv_sem=recv, device_id=device, device_id_type=MESH)


def places():
    row, col = lax.axis_index("row"), lax.axis_index("col")
    rows, cols = lax.axis_size("row"), lax.axis_size("col")
    return row, col, ((row + rows - 1) % rows, col), ((row + 1) % rows, col), (row, (col + cols - 1) % cols), (row, (col + 1) % cols)


def greet(devices):
    barrier = pltpu.get_barrier_semaphore()
    for device in devices:
        pl.semaphore_signal(barrier, inc=1, device_id=device, device_id_type=MESH)
    return barrier


def halo_kernel(tile, probe, meas, th, tl, ext, probev, measv, thv, tlv, g0, pg0, hop1, hop2, zg, zp, loc, snd, rcv):
    row, col, up, down, left, right = places()
    loads = []

    def load(src, dst):
        c = pltpu.make_async_copy(src, dst, loc.at[len(loads)])
        loads.append(c)
        c.start()

    barrier = greet((right, up, down))
    pl.semaphore_wait(barrier, 3)
    n = [0]
    sent = []

    def send(src, dst, device):
        k = n[0]
        n[0] += 1
        c = put(src, dst, snd.at[k], rcv.at[k], device)
        c.start()
        sent.append(c)
        return c

    def lanes(cb):
        return pl.ds(128 * cb, 128)

    H = W // 2
    low = pl.ds(T, W)
    far = [pl.ds(T + H * k, H) for k in range(2)]
    first = [send(tile.at[:, pl.ds(H * k, H), lanes(3)], hop1.at[k], down) for k in range(2)]
    b = [send(tile.at[:, pl.ds(0, W), lanes(cb)], ext.at[:, cb, low, :], up) for cb in range(2)]
    r = [send(tile.at[:, :, lanes(cb)], ext.at[:, 4 + cb, pl.ds(0, T), :], left) for cb in range(2)]
    b2 = send(tile.at[:, pl.ds(0, W), lanes(2)], ext.at[:, 2, low, :], up)
    for cb in range(4):
        load(tile.at[:, :, lanes(cb)], ext.at[:, cb, pl.ds(0, T), :])
    for src, dst in ((probe, probev), (meas, measv), (th, thv), (tl, tlv)):
        load(src, dst)
    zg[...] = jnp.zeros_like(zg)
    zp[...] = jnp.zeros_like(zp)
    for cb in range(6):
        load(zg, g0.at[:, cb])
    load(zp, pg0)
    second, third, x = [], [], []
    for k in range(2):
        first[k].wait_recv()
        second.append(send(hop1.at[k], hop2.at[k], down))
    for k in range(2):
        b[k].wait_recv()
        x.append(send(ext.at[:, k, low, :], ext.at[:, 4 + k, low, :], left))
        second[k].wait_recv()
        third.append(send(hop2.at[k], ext.at[:, 3, far[k], :], down))
    for c in loads:
        c.wait()
    for c in (*r, b2, *third, *x):
        c.wait_recv()
    for c in sent:
        c.wait_send()


def halos(tile, probe, meas, th, tl):
    f = jnp.float32
    A = pl.BlockSpec(memory_space=pl.ANY)
    sd = jax.ShapeDtypeStruct
    H = W // 2
    same = [sd(a.shape, a.dtype) for a in (probe, meas, th, tl)]
    return pl.pallas_call(lambda *a: halo_kernel(*a), out_shape=[sd((2, 6, T + W, 128), f), *same, sd((2, 6, T + W, 128), f), sd((3, W, W), f)],
        in_specs=[pl.BlockSpec(memory_space=pltpu.HBM)] * 5, out_specs=[A] * 7,
        scratch_shapes=[pltpu.VMEM((2, 2, H, 128), f), pltpu.VMEM((2, 2, H, 128), f), pltpu.VMEM((2, T + W, 128), f), pltpu.VMEM((3, W, W), f), pltpu.SemaphoreType.DMA((16,)), pltpu.SemaphoreType.DMA((13,)), pltpu.SemaphoreType.DMA((13,))],
        compiler_params=pltpu.CompilerParams(collective_id=0, has_side_effects=True, vmem_limit_bytes=VM1*2**20))(*[pltpu.with_memory_space_constraint(a, pltpu.HBM) for a in (tile, probe, meas, th, tl)])


GIVE = ((0, 1), (2,), (3,))


def spill_kernel(g, pg, rrv, brv, step, hop1, hop2, zhop1, zhop2, corner, bleft, mine, half, acc, plane, part, ybuf, shard, loc, snd, rcv, psnd, prcv, gsnd, grcv, fsnd, frcv, zsnd, zrcv):
    row, col, up, down, left, right = places()
    rows, depth = lax.axis_size("row"), 4
    chips = lax.axis_size("col") // 2
    wide = chips // depth
    core, chip = col % 2, col // 2
    x, z = chip // depth, chip % depth
    H = W // 2
    step_rows = H // chips

    def at(xx, zz, cc):
        return (row, ((xx % wide) * depth + zz % depth) * 2 + cc)

    def peer(j):
        return (row, ((chip + j) % chips) * 2 + core)

    sib = at(x, z, 1 - core)
    zm = at(x, z + depth - 1, core)
    turn = at(x + jnp.where(z == 2, 1, 0), z + depth - 1, 1)
    around = at(x, z + depth - 1, 0)
    source = at(x, z + 1, 1)
    ys = [((row + k) % rows, col) for k in range(1, 4)]
    barrier = greet((left, sib, *ys))

    @pl.when(core == 0)
    def _():
        pl.semaphore_signal(barrier, inc=1, device_id=source, device_id_type=MESH)

    def hello(j, _):
        pl.semaphore_signal(barrier, inc=1, device_id=peer(j), device_id_type=MESH)
        return 0

    lax.fori_loop(1, chips, hello, 0)
    loads = []

    def load(src, dst):
        c = pltpu.make_async_copy(src, dst, loc.at[len(loads)])
        loads.append(c)
        c.start()
        return c

    def block(start, size):
        return pl.ds(pl.multiple_of(start, size), size)

    low, top = pl.ds(T, W), pl.ds(0, T)
    l_mine = load(pg.at[:, block(core * H, H), :], mine)
    l_left = load(g.at[:, pl.ds(0, 2), low, :], bleft)
    pl.semaphore_wait(barrier, 5 + chips - 1 + core)
    n = [0]
    sent = []

    def send(src, dst, device):
        k = n[0]
        n[0] += 1
        c = put(src, dst, snd.at[k], rcv.at[k], device)
        c.start()
        sent.append(c)
        return c

    s1 = send(pg.at[:, block((1 - core) * H, H), :], half, sib)
    cuts = [pl.ds(NC * k, NC) for k in range(W // NC)]
    sc = [send(g.at[:, 4:6, pl.ds(T + NC * k, NC), :], corner.at[:, :, cuts[k], :], right) for k in range(W // NC)]
    far = [pl.ds(H * k, H) for k in range(2)]
    first = [send(g.at[:, 3, pl.ds(T + H * k, H), :], hop1.at[k], up) for k in range(2)]
    b2 = send(g.at[:, 2, low, :], brv.at[:, 2], down)
    zrows = [pl.ds(H * (k + 1), H) for k in range(3)]

    def zcopy(level, k):
        if level == 0:
            return put(g.at[:, 5, zrows[k], :], zhop1.at[k], zsnd.at[k], zrcv.at[k], zm)
        if level == 1:
            return put(zhop1.at[k], zhop2.at[k], zsnd.at[3 + k], zrcv.at[3 + k], turn)
        return put(zhop2.at[k], rrv.at[:, 1, zrows[k], :], zsnd.at[6 + k], zrcv.at[6 + k], around)

    def zdirect(k):
        return put(g.at[:, 5, zrows[k], :], rrv.at[:, 1, zrows[k], :], zsnd.at[k], zrcv.at[6 + k], sib)

    l_mine.wait()
    s1.wait_recv()
    acc[...] = mine[...] + half[...]

    def shard_of(j):
        p = (chip + j) % chips
        return put(acc.at[:, block(p * step_rows, step_rows), :], plane.at[j], psnd.at[j], prcv.at[j], peer(j))

    def begin(j, _):
        shard_of(j).start()
        return 0

    lax.fori_loop(1, chips, begin, 0)
    @pl.when(core == 1)
    def _():
        for k in range(3):
            zcopy(0, k).start()

    @pl.when(core == 0)
    def _():
        for k in range(3):
            zdirect(k).start()

    r = [send(g.at[:, 4, top, :], rrv.at[:, 0], right), send(g.at[:, 5, pl.ds(0, H), :], rrv.at[:, 1, pl.ds(0, H), :], right)]
    l_left.wait()
    b, second, third = [], [], []
    def give(k):
        sc[k].wait_recv()
        bleft[:, :, cuts[k], :] += corner[:, :, cuts[k], :]
        b.append(send(bleft.at[:, :, cuts[k], :], brv.at[:, 0:2, cuts[k], :], down))

    for k in GIVE[0]:
        give(k)
    for j in range(2):
        first[j].wait_recv()
        second.append(send(hop1.at[j], hop2.at[j], up))

    @pl.when(core == 1)
    def _():
        for k in range(3):
            zcopy(0, k).wait_recv()
            zcopy(1, k).start()

    part[...] = acc[:, block(chip * step_rows, step_rows), :]

    def collect(j, _):
        shard_of(j).wait_recv()
        part[...] += plane[j]
        return 0

    lax.fori_loop(1, chips, collect, 0)
    yr = [send(part, ybuf.at[row], ys[k]) for k in range(3)]
    ybuf[pl.ds(row, 1)] = part[...][None]
    for k in GIVE[1]:
        give(k)
    for c in yr:
        c.wait_recv()
    total = ybuf[0] + ybuf[1] + ybuf[2] + ybuf[3]
    shard[...] = total[:2] / jnp.sqrt(total[2:])
    here = block(core * H + chip * step_rows, step_rows)

    own = load(shard, step.at[:, here, :])

    def gather(j):
        return put(shard, step.at[:, here, :], gsnd.at[j], grcv.at[j], peer(j))

    def begin2(j, _):
        gather(j).start()
        return 0

    lax.fori_loop(1, chips, begin2, 0)

    def pass_on(j):
        rows_j = block(core * H + (chip + chips - j) % chips * step_rows, step_rows)
        return put(step.at[:, rows_j, :], step.at[:, rows_j, :], fsnd.at[j], frcv.at[j], sib)

    own.wait()
    pass_on(0).start()
    for k in GIVE[2]:
        give(k)
    for k in range(2):
        second[k].wait_recv()
        third.append(send(hop2.at[k], brv.at[:, 3, far[k], :], up))

    @pl.when(core == 1)
    def _():
        for k in range(3):
            zcopy(1, k).wait_recv()
            zcopy(2, k).start()


    def collect2(j, _):
        gather(j).wait_recv()
        pass_on(j).start()
        return 0

    lax.fori_loop(1, chips, collect2, 0)
    for c in (*r, b2, *b, *third):
        c.wait_recv()
    for k in range(3):
        zcopy(2, k).wait_recv()

    def collect3(j, _):
        pass_on(j).wait_recv()
        pass_on(j).wait_send()
        return 0

    lax.fori_loop(0, chips, collect3, 0)

    def drain(j, _):
        shard_of(j).wait_send()
        gather(j).wait_send()
        return 0

    lax.fori_loop(1, chips, drain, 0)
    for c in sent:
        c.wait_send()

    @pl.when(core == 1)
    def _():
        for level in range(3):
            for k in range(3):
                zcopy(level, k).wait_send()

    @pl.when(core == 0)
    def _():
        for k in range(3):
            zdirect(k).wait_send()


def spills(g, pg, rows, cols):
    f = jnp.float32
    A = pl.BlockSpec(memory_space=pl.ANY)
    sd = jax.ShapeDtypeStruct
    V = pltpu.VMEM
    D = pltpu.SemaphoreType.DMA
    H = W // 2
    chips = cols // 2
    sh = H // chips
    return pl.pallas_call(lambda *a: spill_kernel(*a), out_shape=[sd((2, 2, T, 128), f), sd((2, 4, W, 128), f), sd((2, W, W), f)],
        in_specs=[A] * 2, out_specs=[A] * 3,
        scratch_shapes=[V((2, 2, H, 128), f), V((2, 2, H, 128), f), V((3, 2, H, 128), f), V((3, 2, H, 128), f), V((2, 2, W, 128), f), V((2, 2, W, 128), f),
            V((3, H, W), f), V((3, H, W), f), V((3, H, W), f), V((chips, 3, sh, W), f), V((3, sh, W), f), V((rows, 3, sh, W), f), V((2, sh, W), f),
            D((4,)), D((40,)), D((40,)), *[D((chips,))] * 6, D((9,)), D((9,))],
        compiler_params=pltpu.CompilerParams(collective_id=1, has_side_effects=True, vmem_limit_bytes=VM3*2**20))(g, pg)


def join_kernel(g, rrv, brv, stepv, grad, step, out, sem):
    s = pltpu.make_async_copy(stepv, step, sem.at[4])
    s.start()
    cps = []
    for cb in (3, 2, 1, 0):
        for k in range(4):
            at_rows = pl.ds(128 * k, 128)
            v = g[:, cb, at_rows, :]
            if cb < 2:
                v = v + rrv[:, cb, at_rows, :]
            if k < 2:
                v = v + brv[:, cb, at_rows, :]
            out[:, cb, at_rows, :] = v
        cps.append(pltpu.make_async_copy(out.at[:, cb], grad.at[:, :, pl.ds(128 * cb, 128)], sem.at[cb]))
        cps[-1].start()
    for c in (s, *cps):
        c.wait()


def join(g, rrv, brv, stepv):
    f = jnp.float32
    V = pl.BlockSpec(memory_space=pltpu.VMEM)
    A = pl.BlockSpec(memory_space=pl.ANY)
    sd = jax.ShapeDtypeStruct
    return pl.pallas_call(join_kernel, out_shape=[sd((2, T, T), f), sd((2, W, W), f)],
        in_specs=[V, V, V, V], out_specs=[A, A],
        scratch_shapes=[pltpu.VMEM((2, 4, T, 128), f), pltpu.SemaphoreType.DMA((5,))],
        compiler_params=pltpu.CompilerParams(vmem_limit_bytes=16*2**20))(g, rrv, brv, stepv)


def local(specimen, probe_field, measured, offsets, live_counts):
    hi, lo = tables()
    ext, probe, meas, hi, lo, g0, pg0 = halos(specimen, probe_field, measured[0, 0], jnp.asarray(hi), jnp.asarray(lo))
    g, pg = compute(offsets, live_counts, ext, probe, meas, hi, lo, g0, pg0)
    rrv, brv, step = spills(g, pg, lax.axis_size("row"), lax.axis_size("col"))
    return tuple(join(g, rrv, brv, step))


def solution(mesh):
    from jax.sharding import PartitionSpec as P
    in_specs = (P(None, "row", "col"), P(), P("row", "col", None, None, None), P("row", "col", None, None), P("row", "col"))
    out_specs = (P(None, "row", "col"), P())
    return jax.shard_map(local, mesh=mesh, in_specs=in_specs, out_specs=out_specs, check_vma=False)
```
